128 devices in a mesh: batch: 32 (over y, z_hi, x), feat: 4 (over z_lo, core).
Axes of the slice: x: 4, y: 4, z: 4 (z_hi: 2, z_lo: 2; z = z_hi * 2 + z_lo), core: 2. Of those that a mesh axis runs over, the one named last changes fastest.
Arguments:
- view_a: bfloat16 [16384, 4096], P('batch', 'feat')
- view_b: bfloat16 [16384, 4096], P('batch', 'feat')
Outputs:
- grad_a: float32 [16384, 4096], P('batch', 'feat')
- grad_b: float32 [16384, 4096], P('batch', 'feat')
- loss: float32 [], replicated
All inputs are finite; a program needn't handle non-finite values.
Results may differ from the reference program's by a relative error of at most 0.019.
Values may be sent and summed in bfloat16 or wider, within the bound.
A program may use at most 128 MiB of HBM per device.

```python
import jax
import jax.numpy as jnp
from jax import lax

F = 4096
BATCH = 16384


def shared_base(key):
    return jax.random.normal(key, (BATCH, F), jnp.float32)


def feature_affine(key, spread):
    scale_key, shift_key = jax.random.split(key)
    scales = jnp.exp(jax.random.uniform(scale_key, (F,), jnp.float32, -0.7, 1.4))
    shifts = jax.random.uniform(shift_key, (F,), jnp.float32, -spread, spread)
    return (scales, shifts)


def draw_view_a(key, part):
    base = shared_base(key)
    key = jax.random.fold_in(key, 11)
    scales, shifts = feature_affine(key, 1.0)
    return (base * scales + shifts).astype(jnp.bfloat16)


def draw_view_b(key, part):
    base = shared_base(key)
    key = jax.random.fold_in(key, 23)
    noise_key, mix_key, affine_key = jax.random.split(key, 3)
    noise = jax.random.normal(noise_key, (BATCH, F), jnp.float32)
    scales, shifts = feature_affine(affine_key, 1.0)
    mixing = jnp.exp(jax.random.uniform(mix_key, (F,), jnp.float32, -3.5, -0.9))
    mixed = base * jnp.sqrt(1.0 - mixing * mixing) + noise * mixing
    return (mixed * scales + shifts).astype(jnp.bfloat16)


def setup_inputs(seed: int = 0) -> dict:
    arg_keys = jax.random.split(jax.random.key(seed), 3)
    view_a = draw_view_a(jax.random.fold_in(arg_keys[2], 71), 0)
    view_b = draw_view_b(jax.random.fold_in(arg_keys[2], 71), 0)
    return {"view_a": view_a, "view_b": view_b}


lam_off = 0.0051
eps_norm = 1e-05

def normalize(view):
    values = view.astype(jnp.float32)
    mean_v = lax.optimization_barrier(jnp.mean(values, axis=0))
    var_v = lax.optimization_barrier(jnp.mean((values - mean_v) ** 2, axis=0))
    inv_v = 1.0 / jnp.sqrt(var_v + eps_norm)
    return (((values - mean_v) * inv_v).astype(jnp.bfloat16), inv_v)

def back_norm(back, normed, inv_v):
    nfloat = normed.astype(jnp.float32)
    return inv_v * (back - lax.optimization_barrier(jnp.mean(back, axis=0)) - nfloat * lax.optimization_barrier(jnp.mean(back * nfloat, axis=0)))

def reference(view_a, view_b):
    norm_a, inv_a = normalize(view_a)
    norm_b, inv_b = normalize(view_b)
    corr = jnp.dot(norm_a.T, norm_b, preferred_element_type=jnp.float32) / BATCH
    diag_mask = jnp.eye(F, dtype=bool)
    loss = jnp.sum(jnp.where(diag_mask, (1.0 - corr) ** 2, lam_off * corr * corr))
    gmat = jnp.where(diag_mask, -2.0 * (1.0 - corr), 2.0 * lam_off * corr).astype(jnp.bfloat16)
    back_a = jnp.dot(norm_b, gmat.T, preferred_element_type=jnp.float32)
    back_b = jnp.dot(norm_a, gmat, preferred_element_type=jnp.float32)
    return (back_norm(back_a, norm_a, inv_a), back_norm(back_b, norm_b, inv_b), loss)
```

```python
import functools

import jax
import jax.numpy as jnp
from jax import lax
from jax.experimental import pallas as pl
from jax.experimental.pallas import tpu as pltpu
from jax.sharding import PartitionSpec as P

lam_off = 0.0051
eps_norm = 1e-05
f32 = jnp.float32
bf16 = jnp.bfloat16
MESH = pl.DeviceIdType.MESH

ROWS = 512
FB = 1024
W = 1024
CPK = FB // W
NCH = 4 * CPK
TOTAL = 16384


def column_sum(fn, rows, step=32):
    def body(i, acc):
        v = fn(pl.ds(pl.multiple_of(i * step, step), step))
        return acc + jnp.sum(v.reshape(step // 8, 8, v.shape[-1]), axis=0)

    acc = lax.fori_loop(0, rows // step, body, jnp.zeros((8, FB), f32))
    return jnp.sum(acc, axis=0, keepdims=True)


def kernel(
    a_ref, b_ref, ga_ref, gb_ref, loss_ref,
    na, nat, bn, braw, sb, ld1, sb2, ld2, ub, zl_buf, gt, pbs, pbl,
    ex_x, ex_y, ex_z, lo_x, lo_y, lo_f, vec, lacc,
    ss1, rs1, ss2, rs2, ssz, rsz, ssg2, rsg2, ssg1, rsg1, ssb, rsb, ssp, rsp,
    sse, rse, ssl, rsl,
):
    bi = lax.axis_index("batch")
    fi = lax.axis_index("feat")
    y, zh, x = bi // 8, (bi // 4) % 2, bi % 4
    zl, core = fi // 2, fi % 2

    def dev(y_, zh_, x_, zl_, c_):
        return (((y_ + 4) % 4) * 8 + zh_ * 4 + ((x_ + 4) % 4), zl_ * 2 + c_)

    xdev = {d: dev(y, zh, x + d, zl, core) for d in (1, 2, 3)}
    ydev = {d: dev(y + d, zh, x, zl, core) for d in (1, 2, 3)}
    zhdev = dev(y, 1 - zh, x, zl, core)
    fdev = {1: dev(y, zh, x, zl, 1 - core), 2: dev(y, zh, x, 1 - zl, core),
            3: dev(y, zh, x, 1 - zl, 1 - core)}

    bar = pltpu.get_barrier_semaphore()
    partners = list(xdev.values()) + list(ydev.values()) + [zhdev] + list(fdev.values())
    for q in partners:
        pl.semaphore_signal(bar, inc=1, device_id=q, device_id_type=MESH)
    pl.semaphore_wait(bar, len(partners))

    pending = []

    def send(src, dst, s, r, to):
        cp = pltpu.make_async_remote_copy(
            src_ref=src, dst_ref=dst, send_sem=s, recv_sem=r, device_id=to, device_id_type=MESH)
        cp.start()
        pending.append(cp)

    def arrived(region, s, r):
        pltpu.make_async_remote_copy(
            src_ref=region, dst_ref=region, send_sem=s, recv_sem=r, device_id=zhdev,
            device_id_type=MESH).wait_recv()

    NB = 2
    RB = ROWS // NB
    for i in range(NB):
        rr = pl.ds(i * RB, RB)
        send(b_ref.at[rr], braw.at[0, rr], ssb.at[0, i], rsb.at[0, i], fdev[1])
        send(b_ref.at[rr], braw.at[1, rr], ssb.at[1, i], rsb.at[1, i], fdev[2])

    def forward_raw():
        for i in range(NB):
            rr = pl.ds(i * RB, RB)
            arrived(braw.at[1, rr], ssb.at[1, i], rsb.at[1, i])
            send(braw.at[1, rr], braw.at[2, rr], ssb.at[2, i], rsb.at[2, i], fdev[1])

    def raw_arrived(k):
        if k in (1, 3):
            for i in range(NB):
                rr = pl.ds(i * RB, RB)
                arrived(braw.at[k - 1, rr], ssb.at[k - 1, i], rsb.at[k - 1, i])

    def stage_send(buf, me, peers, base, s, r):
        for i, to in enumerate(peers):
            send(buf.at[me], buf.at[me], s.at[base + i], r.at[base + i], to)

    def stage_wait(buf, froms, base, s, r):
        for i, q in enumerate(froms):
            arrived(buf.at[q], s.at[base + i], r.at[base + i])

    xfrom = [(x + 4 - d) % 4 for d in (1, 2, 3)]
    yfrom = [(y + 4 - d) % 4 for d in (1, 2, 3)]
    xto = [xdev[d] for d in (1, 2, 3)]
    yto = [ydev[d] for d in (1, 2, 3)]

    def ex_parts(e):
        bx, by, bz = ex_x.at[e], ex_y.at[e], ex_z.at[e]
        s, r = sse.at[e], rse.at[e]
        return bx, by, bz, s, r

    def ex_start(e, value):
        bx, by, bz, s, r = ex_parts(e)
        bx[x] = value
        stage_send(bx, x, xto, 0, s, r)

    def ex_mid(e, merge):
        bx, by, bz, s, r = ex_parts(e)
        stage_wait(bx, xfrom, 0, s, r)
        by[y] = merge([bx[q] for q in range(4)], ROWS)
        stage_send(by, y, yto, 3, s, r)

    def ex_last(e, merge):
        bx, by, bz, s, r = ex_parts(e)
        stage_wait(by, yfrom, 3, s, r)
        bz[zh] = merge([by[q] for q in range(4)], ROWS * 4)
        stage_send(bz, zh, [zhdev], 6, s, r)

    def ex_end(e, merge):
        bx, by, bz, s, r = ex_parts(e)
        stage_wait(bz, [1 - zh], 6, s, r)
        return merge([bz[0], bz[1]], ROWS * 16)

    def merge_sum(vs, n):
        t = vs[0]
        for v in vs[1:]:
            t = t + v
        return t

    def merge_moments(vs, n):
        mean = merge_sum(vs, n)[0:2] * (1.0 / len(vs))
        m2 = merge_sum(vs, n)[2:4]
        for v in vs:
            d = v[0:2] - mean
            m2 = m2 + float(n) * d * d
        return jnp.concatenate([mean, m2, jnp.zeros((4, FB), f32)], axis=0)

    mean_a = column_sum(lambda s: a_ref[s].astype(f32), ROWS) * (1.0 / ROWS)
    mean_b = column_sum(lambda s: b_ref[s].astype(f32), ROWS) * (1.0 / ROWS)

    def dev2(ref, mean):
        def f(s):
            d = ref[s].astype(f32) - mean
            return d * d
        return column_sum(f, ROWS)

    m2_a = dev2(a_ref, mean_a)
    m2_b = dev2(b_ref, mean_b)
    ex_start(0, jnp.concatenate([mean_a, mean_b, m2_a, m2_b, jnp.zeros((4, FB), f32)], axis=0))
    ex_mid(0, merge_moments)
    ex_last(0, merge_moments)
    st = ex_end(0, merge_moments)
    inv = 1.0 / jnp.sqrt(st[2:4] * (1.0 / TOTAL) + eps_norm)
    vec[0] = jnp.concatenate([st[0:2], inv, jnp.zeros((4, FB), f32)], axis=0)
    for k in (1, 2, 3):
        send(vec.at[0], vec.at[k], ssb.at[3, k - 1], rsb.at[3, k - 1], fdev[k])

    def normalise(src, dst, mean, iv):
        def body(i, _):
            s = pl.ds(pl.multiple_of(i * 64, 64), 64)
            dst[s, :] = ((src[s, :].astype(f32) - mean) * iv).astype(bf16)
            return 0
        lax.fori_loop(0, ROWS // 64, body, 0)

    normalise(a_ref, na, st[0:1], inv[0:1])
    normalise(b_ref, bn.at[0], st[1:2], inv[1:2])
    for i in range(4):
        nat[pl.ds(i * 256, 256), :] = na[:, pl.ds(i * 256, 256)].T
    dsum = column_sum(lambda s: na[s].astype(f32) * bn[0, s].astype(f32), ROWS)
    ex_start(1, jnp.concatenate([dsum, jnp.zeros((7, FB), f32)], axis=0))
    lacc[...] = jnp.zeros_like(lacc)

    def prepare(k):
        if k == 0:
            return
        raw_arrived(k)
        arrived(vec.at[k], ssb.at[3, k - 1], rsb.at[3, k - 1])
        v = vec[k]
        normalise(braw.at[k - 1], bn.at[k], v[1:2], v[3:4])

    p1 = (x, y)
    p2 = (y, x)
    right1, left1 = (xdev[1], ydev[1]), (xdev[3], ydev[3])
    right2, left2 = (ydev[1], xdev[1]), (ydev[3], xdev[3])

    def at(q, d):
        return (q + d) % 4

    def piece(base, q, size, lo, n):
        return pl.ds(pl.multiple_of(base + q * size + lo, 16), n)

    def ring_early(buf, land, base, q, size, right, left, s, r):
        hf = size // 2
        send(buf.at[piece(base, at(q, 2), size, 0, hf)], land.at[0], s.at[0], r.at[0], right)
        send(buf.at[piece(base, at(q, 2), size, hf, hf)], land.at[1], s.at[1], r.at[1], left)
        send(buf.at[piece(base, at(q, 1), size, hf, hf)], land.at[2], s.at[2], r.at[2], right)
        send(buf.at[piece(base, at(q, 3), size, 0, hf)], land.at[3], s.at[3], r.at[3], left)

    def ring_late(buf, land, base, q, size, right, left, s, r):
        hf = size // 2
        ra = piece(base, at(q, 1), size, 0, hf)
        lb = piece(base, at(q, 3), size, hf, hf)
        arrived(land.at[0], s.at[0], r.at[0])
        buf[ra, :] = (buf[ra, :].astype(f32) + land[0].astype(f32)).astype(bf16)
        send(buf.at[ra], land.at[4], s.at[4], r.at[4], right)
        arrived(land.at[1], s.at[1], r.at[1])
        buf[lb, :] = (buf[lb, :].astype(f32) + land[1].astype(f32)).astype(bf16)
        send(buf.at[lb], land.at[5], s.at[5], r.at[5], left)

    def ring_fin(buf, land, base, q, size, out, obase, s, r):
        hf = size // 2
        for m in (2, 3, 4, 5):
            arrived(land.at[m], s.at[m], r.at[m])
        ha = piece(base, q, size, 0, hf)
        hb = piece(base, q, size, hf, hf)
        out[pl.ds(obase, hf), :] = (
            buf[ha, :].astype(f32) + land[3].astype(f32) + land[4].astype(f32)).astype(bf16)
        out[pl.ds(obase + hf, hf), :] = (
            buf[hb, :].astype(f32) + land[2].astype(f32) + land[5].astype(f32)).astype(bf16)

    def gather_early(buf, base, q, size, right, left, s, r):
        own = buf.at[piece(base, q, size, 0, size)]
        send(own, own, s.at[0], r.at[0], right)
        send(own, own, s.at[1], r.at[1], left)

    def gather_late(buf, base, q, size, right, left, s, r):
        hf = size // 2
        fl = buf.at[piece(base, at(q, 3), size, 0, size)]
        fr = buf.at[piece(base, at(q, 1), size, 0, size)]
        arrived(fl, s.at[0], r.at[0])
        ha = buf.at[piece(base, at(q, 3), size, 0, hf)]
        send(ha, ha, s.at[2], r.at[2], right)
        arrived(fr, s.at[1], r.at[1])
        hb = buf.at[piece(base, at(q, 1), size, hf, hf)]
        send(hb, hb, s.at[3], r.at[3], left)

    def gather_fin(buf, base, q, size, s, r):
        hf = size // 2
        arrived(buf.at[piece(base, at(q, 2), size, 0, hf)], s.at[2], r.at[2])
        arrived(buf.at[piece(base, at(q, 2), size, hf, hf)], s.at[3], r.at[3])

    def blk(c):
        return c // CPK

    def col(c):
        return (c % CPK) * W

    def t_dot(c):
        k = blk(c)
        if c % CPK == 0:
            prepare(k)
        n = 256

        def body(j, _):
            o = pl.multiple_of(j * n, n)
            i = pl.multiple_of(col(c) + j * n, n)
            sb[c, :, pl.ds(o, n)] = jnp.dot(
                nat[...], bn[k, :, pl.ds(i, n)], preferred_element_type=f32).astype(bf16)
            return 0

        lax.fori_loop(0, W // n, body, 0)
        for h in (0, 1):
            ring_early(sb.at[c], ld1.at[c, h], 512 * h, p1[h], 128, right1[h], left1[h],
                       ss1.at[c, h], rs1.at[c, h])

    def t_late1(c):
        for h in (0, 1):
            ring_late(sb.at[c], ld1.at[c, h], 512 * h, p1[h], 128, right1[h], left1[h],
                      ss1.at[c, h], rs1.at[c, h])

    def t_fin1(c):
        for h in (0, 1):
            ring_fin(sb.at[c], ld1.at[c, h], 512 * h, p1[h], 128, sb2.at[c, h], 0,
                     ss1.at[c, h], rs1.at[c, h])
            ring_early(sb2.at[c, h], ld2.at[c, h], 0, p2[h], 32, right2[h], left2[h],
                       ss2.at[c, h], rs2.at[c, h])

    def t_late2(c):
        for h in (0, 1):
            ring_late(sb2.at[c, h], ld2.at[c, h], 0, p2[h], 32, right2[h], left2[h],
                      ss2.at[c, h], rs2.at[c, h])

    def t_fin2(c):
        for h in (0, 1):
            ring_fin(sb2.at[c, h], ld2.at[c, h], 0, p2[h], 32, ub.at[c], 32 * h,
                     ss2.at[c, h], rs2.at[c, h])
        send(ub.at[c], zl_buf.at[c], ssz.at[c], rsz.at[c], zhdev)

    def t_tile(c):
        arrived(zl_buf.at[c], ssz.at[c], rsz.at[c])
        for h in (0, 1):
            base = 512 * h + 128 * p1[h] + 32 * p2[h]
            corr = (ub[c, pl.ds(32 * h, 32), :].astype(f32)
                    + zl_buf[c, pl.ds(32 * h, 32), :].astype(f32)) * (1.0 / TOTAL)
            if blk(c) == 0:
                diag = vec[4, 0:1, pl.ds(col(c), W)]
                rows = base + lax.broadcasted_iota(jnp.int32, (32, W), 0)
                cols = col(c) + lax.broadcasted_iota(jnp.int32, (32, W), 1)
                on = rows == cols
                gap = jnp.broadcast_to(1.0 - diag, (32, W))
                l = jnp.where(on, gap * gap, lam_off * corr * corr)
                g = jnp.where(on, -2.0 * gap, 2.0 * lam_off * corr)
            else:
                l = lam_off * corr * corr
                g = 2.0 * lam_off * corr
            lacc[...] += jnp.sum(l.reshape(4, 8, W), axis=0)
            gt[c, pl.ds(pl.multiple_of(base, 32), 32), :] = g.astype(bf16)
        for h in (0, 1):
            gather_early(gt.at[c], 512 * h + 128 * p1[h], p2[h], 32, right2[h], left2[h],
                         ssg2.at[c, h], rsg2.at[c, h])

    def t_fwd2(c):
        for h in (0, 1):
            gather_late(gt.at[c], 512 * h + 128 * p1[h], p2[h], 32, right2[h], left2[h],
                        ssg2.at[c, h], rsg2.at[c, h])

    def t_gat1(c):
        for h in (0, 1):
            gather_fin(gt.at[c], 512 * h + 128 * p1[h], p2[h], 32, ssg2.at[c, h], rsg2.at[c, h])
            gather_early(gt.at[c], 512 * h, p1[h], 128, right1[h], left1[h],
                         ssg1.at[c, h], rsg1.at[c, h])

    def t_fwd1(c):
        for h in (0, 1):
            gather_late(gt.at[c], 512 * h, p1[h], 128, right1[h], left1[h],
                        ssg1.at[c, h], rsg1.at[c, h])

    started = []

    def t_back(c):
        k = blk(c)
        n = 256
        for h in (0, 1):
            gather_fin(gt.at[c], 512 * h, p1[h], 128, ssg1.at[c, h], rsg1.at[c, h])
        first = not started
        started.append(c)

        if c % CPK == 0 and k == 2:
            pass

        def body_b(j, _):
            o = pl.multiple_of(j * n, n)
            i = pl.multiple_of(col(c) + j * n, n)
            v = jnp.dot(na[...], gt[c, :, pl.ds(o, n)], preferred_element_type=f32)
            if k == 0:
                gb_ref[:, pl.ds(i, n)] = v
            elif k == 2:
                pbs[1, :, pl.ds(i, n)] = (
                    v + pbl[2, :, pl.ds(i, n)].astype(f32)).astype(bf16)
            else:
                pbs[k - 1, :, pl.ds(i, n)] = v.astype(bf16)
            return 0

        cs = pl.ds(col(c), W)
        if k == 2:
            arrived(pbl.at[2, :, cs], ssp.at[2, c % CPK], rsp.at[2, c % CPK])
        lax.fori_loop(0, W // n, body_b, 0)
        if k != 0:
            to = fdev[2] if k == 2 else fdev[1]
            send(pbs.at[k - 1, :, cs], pbl.at[k - 1, :, cs],
                 ssp.at[k - 1, c % CPK], rsp.at[k - 1, c % CPK], to)

        def body_a(j, _):
            o = pl.multiple_of(j * n, n)
            v = lax.dot_general(bn[k, :, cs], gt[c, pl.ds(o, n), :], (((1,), (1,)), ((), ())),
                                preferred_element_type=f32)
            if first:
                ga_ref[:, pl.ds(o, n)] = v
            else:
                ga_ref[:, pl.ds(o, n)] += v
            return 0

        lax.fori_loop(0, FB // n, body_a, 0)

    def diag_done():
        d = ex_end(1, merge_sum)
        vec[4] = d * (1.0 / TOTAL)

    def loss_start():
        lo_x[x] = lacc[...]
        stage_send(lo_x, x, xto, 0, ssl, rsl)

    def loss_mid():
        stage_wait(lo_x, xfrom, 0, ssl, rsl)
        lo_y[y] = merge_sum([lo_x[q] for q in range(4)], 0)
        stage_send(lo_y, y, yto, 3, ssl, rsl)

    def loss_feat():
        stage_wait(lo_y, yfrom, 3, ssl, rsl)
        lo_f[fi] = merge_sum([lo_y[q] for q in range(4)], 0)
        stage_send(lo_f, fi, [fdev[1], fdev[2], fdev[3]], 6, ssl, rsl)

    def loss_end():
        stage_wait(lo_f, [fi + 1 - 2 * core, (fi + 2) % 4, (fi + 2) % 4 + 1 - 2 * core], 6, ssl, rsl)
        t = merge_sum([lo_f[q] for q in range(4)], 0)
        loss_ref[...] = jnp.full((8, 128), jnp.sum(t), f32)

    t_dot(0)
    ex_mid(1, merge_sum)
    t_late1(0)
    ex_last(1, merge_sum)
    t_dot(1)
    t_fin1(0)
    diag_done()
    t_late1(1)
    forward_raw()
    t_late2(0)
    t_dot(2)
    t_fin2(0)
    t_fin1(1)
    t_late1(2)
    t_dot(3)
    t_late2(1)
    t_fin1(2)
    t_fin2(1)
    t_late1(3)
    t_late2(2)
    t_fin1(3)
    t_fin2(2)
    t_tile(2)
    t_late2(3)
    t_fwd2(2)
    t_fin2(3)
    t_tile(0)
    t_tile(1)
    t_gat1(2)
    t_tile(3)
    t_fwd1(2)
    t_fwd2(3)
    loss_start()
    t_gat1(3)
    t_fwd2(0)
    t_fwd2(1)
    t_fwd1(3)
    t_gat1(0)
    loss_mid()
    t_gat1(1)
    t_back(3)
    t_fwd1(0)
    t_back(2)
    loss_feat()
    t_fwd1(1)
    t_back(1)
    t_back(0)
    loss_end()

    for j in range(CPK):
        cs = pl.ds(j * W, W)
        arrived(pbl.at[0, :, cs], ssp.at[0, j], rsp.at[0, j])
        arrived(pbl.at[1, :, cs], ssp.at[1, j], rsp.at[1, j])

    def add_b(i, acc):
        s = pl.ds(pl.multiple_of(i * 32, 32), 32)
        v = gb_ref[s, :] + pbl[0, s, :].astype(f32) + pbl[1, s, :].astype(f32)
        gb_ref[s, :] = v
        u = ga_ref[s, :]
        fold = lambda t: jnp.sum(t.reshape(4, 8, FB), axis=0)
        return (acc[0] + fold(u), acc[1] + fold(u * na[s, :].astype(f32)),
                acc[2] + fold(v), acc[3] + fold(v * bn[0, s, :].astype(f32)))

    z8 = jnp.zeros((8, FB), f32)
    acc = lax.fori_loop(0, ROWS // 32, add_b, (z8, z8, z8, z8))
    ex_start(2, jnp.concatenate([jnp.sum(t, axis=0, keepdims=True) for t in acc]
                                + [jnp.zeros((4, FB), f32)], axis=0))
    ex_mid(2, merge_sum)
    ex_last(2, merge_sum)
    m = ex_end(2, merge_sum) * (1.0 / TOTAL)
    iv = vec[0]

    def finish(i, _):
        s = pl.ds(pl.multiple_of(i * 32, 32), 32)
        ga_ref[s, :] = iv[2:3] * (ga_ref[s, :] - m[0:1] - na[s, :].astype(f32) * m[1:2])
        gb_ref[s, :] = iv[3:4] * (gb_ref[s, :] - m[2:3] - bn[0, s, :].astype(f32) * m[3:4])
        return 0

    lax.fori_loop(0, ROWS // 32, finish, 0)
    for cp in pending:
        cp.wait_send()


def shards(view_a, view_b):
    vm = pl.BlockSpec(memory_space=pltpu.VMEM)
    dma = pltpu.SemaphoreType.DMA
    scratch = [
        pltpu.VMEM((ROWS, FB), bf16),
        pltpu.VMEM((FB, ROWS), bf16),
        pltpu.VMEM((4, ROWS, FB), bf16),
        pltpu.VMEM((3, ROWS, FB), bf16),
        pltpu.VMEM((NCH, FB, W), bf16),
        pltpu.VMEM((NCH, 2, 6, 64, W), bf16),
        pltpu.VMEM((NCH, 2, 128, W), bf16),
        pltpu.VMEM((NCH, 2, 6, 16, W), bf16),
        pltpu.VMEM((NCH, 64, W), bf16),
        pltpu.VMEM((NCH, 64, W), bf16),
        pltpu.VMEM((NCH, FB, W), bf16),
        pltpu.VMEM((3, ROWS, FB), bf16),
        pltpu.VMEM((3, ROWS, FB), bf16),
        pltpu.VMEM((3, 4, 8, FB), f32),
        pltpu.VMEM((3, 4, 8, FB), f32),
        pltpu.VMEM((3, 2, 8, FB), f32),
        pltpu.VMEM((4, 8, W), f32),
        pltpu.VMEM((4, 8, W), f32),
        pltpu.VMEM((4, 8, W), f32),
        pltpu.VMEM((5, 8, FB), f32),
        pltpu.VMEM((8, W), f32),
        dma((NCH, 2, 6)), dma((NCH, 2, 6)),
        dma((NCH, 2, 6)), dma((NCH, 2, 6)),
        dma((NCH,)), dma((NCH,)),
        dma((NCH, 2, 4)), dma((NCH, 2, 4)),
        dma((NCH, 2, 4)), dma((NCH, 2, 4)),
        dma((4, 4)), dma((4, 4)),
        dma((3, CPK)), dma((3, CPK)),
        dma((3, 7)), dma((3, 7)),
        dma((9,)), dma((9,)),
    ]
    ga, gb, loss = pl.pallas_call(
        kernel,
        out_shape=(
            jax.ShapeDtypeStruct((ROWS, FB), f32),
            jax.ShapeDtypeStruct((ROWS, FB), f32),
            jax.ShapeDtypeStruct((8, 128), f32),
        ),
        in_specs=[vm, vm],
        out_specs=(vm, vm, vm),
        scratch_shapes=scratch,
        compiler_params=pltpu.CompilerParams(
            collective_id=0, has_side_effects=True, vmem_limit_bytes=60 * 2**20),
        name="barlow",
    )(view_a, view_b)
    return ga, gb, loss[0, 0]


def solution(mesh):
    return jax.shard_map(
        shards,
        mesh=mesh,
        in_specs=(P("batch", "feat"), P("batch", "feat")),
        out_specs=(P("batch", "feat"), P("batch", "feat"), P()),
        check_vma=False,
    )
```

```python
import jax
import jax.numpy as jnp
from jax import lax
from jax.experimental import pallas as pl
from jax.experimental.pallas import tpu as pltpu
from jax.sharding import PartitionSpec as P

lam_off = 0.0051
eps_norm = 1e-05
f32 = jnp.float32
bf16 = jnp.bfloat16
MESH = pl.DeviceIdType.MESH

ROWS = 512
RX = ROWS + 16
FB = 1024
CPK = 2
W = FB // CPK
NCH = 4 * CPK
TOTAL = 16384


def column_sum(fn, rows, step=32):
    def body(i, acc):
        v = fn(pl.ds(pl.multiple_of(i * step, step), step))
        return acc + jnp.sum(v.reshape(step // 8, 8, v.shape[-1]), axis=0)

    acc = lax.fori_loop(0, rows // step, body, jnp.zeros((8, FB), f32))
    return jnp.sum(acc, axis=0, keepdims=True)


def fold(v):
    return jnp.concatenate([v[:, : FB // 2], v[:, FB // 2:]], axis=0)


def unfold(v):
    return jnp.concatenate([v[0:4], v[4:8]], axis=1)


def total_of(vs):
    t = vs[0]
    for v in vs[1:]:
        t = t + v
    return t


def merge_moments(vs, n):
    vs = [unfold(v) for v in vs]
    t = total_of(vs)
    mean = t[0:2] * (1.0 / len(vs))
    m2 = t[2:4]
    for v in vs:
        d = v[0:2] - mean
        m2 = m2 + float(n) * d * d
    return jnp.concatenate([mean, m2], axis=0)


def kernel(
    a_ref, b_ref, ga_ref, gb_ref, loss_ref,
    na, nat, bn, braw, sb, ld1, sb2, ld2, ub, zbuf, gt, pbs, pbl, acc_a, acc_b,
    ex, lo, pay, vec, sbv, lacc, racc,
    ss, r1s, r2s, zs, g2s, g1s, bs, vs_, fs, ps, es, ls,
):
    bi = lax.axis_index("batch")
    fi = lax.axis_index("feat")
    y, zh, x = bi // 8, (bi // 4) % 2, bi % 4
    zl, core = fi // 2, fi % 2

    def dev(y_, zh_, x_, zl_, c_):
        return (((y_ + 4) % 4) * 8 + zh_ * 4 + ((x_ + 4) % 4), zl_ * 2 + c_)

    xdev = {d: dev(y, zh, x + d, zl, core) for d in (1, 2, 3)}
    ydev = {d: dev(y + d, zh, x, zl, core) for d in (1, 2, 3)}
    zhdev = dev(y, 1 - zh, x, zl, core)
    fdev = {1: dev(y, zh, x, zl, 1 - core), 2: dev(y, zh, x, 1 - zl, core),
            3: dev(y, zh, x, 1 - zl, 1 - core)}
    fidx = {0: fi, 1: zl * 2 + 1 - core, 2: (1 - zl) * 2 + core, 3: (1 - zl) * 2 + 1 - core}

    bar = pltpu.get_barrier_semaphore()
    partners = list(xdev.values()) + list(ydev.values()) + [zhdev] + list(fdev.values())
    for q in partners:
        pl.semaphore_signal(bar, inc=1, device_id=q, device_id_type=MESH)

    recv = {"r1": r1s, "r2": r2s, "z": zs, "g2": g2s, "g1": g1s, "b": bs, "v": vs_, "f": fs,
            "p": ps, "e": es, "l": ls}
    sent = {name: ss.at[i] for i, name in enumerate(recv)}

    def send(src, dst, key, to):
        cp = pltpu.make_async_remote_copy(
            src_ref=src, dst_ref=dst, send_sem=sent[key[0]], recv_sem=recv[key[0]].at[key[1:]],
            device_id=to, device_id_type=MESH)
        cp.start()

    def await_bytes(region, key):
        pltpu.make_async_remote_copy(
            src_ref=region, dst_ref=region, send_sem=sent[key[0]], recv_sem=recv[key[0]].at[key[1:]],
            device_id=zhdev, device_id_type=MESH).wait_recv()

    def await_sent(region, name):
        pltpu.make_async_remote_copy(
            src_ref=region, dst_ref=region, send_sem=sent[name], recv_sem=sent[name],
            device_id=zhdev, device_id_type=MESH).wait_send()

    mean_a = column_sum(lambda s: a_ref[s].astype(f32), ROWS) * (1.0 / ROWS)
    mean_b = column_sum(lambda s: b_ref[s].astype(f32), ROWS) * (1.0 / ROWS)

    def deviations(ref, mean):
        def f(s):
            d = ref[s].astype(f32) - mean
            return d * d
        return column_sum(f, ROWS)

    moments = jnp.concatenate(
        [mean_a, mean_b, deviations(a_ref, mean_a), deviations(b_ref, mean_b)], axis=0)
    pl.semaphore_wait(bar, len(partners))

    xto = [xdev[d] for d in (1, 2, 3)]
    yto = [ydev[d] for d in (1, 2, 3)]
    axes = {"x": (0, 4, x, xto), "y": (4, 4, y, yto), "z": (8, 2, zh, [zhdev])}

    def ex_send(e, axis, value):
        base, n, me, to = axes[axis]
        ex[e, base + me] = fold(value)
        for q in to:
            send(ex.at[e, base + me], ex.at[e, base + me], ("e", e, base // 4), q)

    def ex_wait(e, axis):
        base, n, me, to = axes[axis]
        await_bytes(ex.at[e, pl.ds(base, n - 1)], ("e", e, base // 4))
        return [ex[e, base + q] for q in range(n)]

    half = ROWS // 2

    def raw0():
        send(b_ref, braw.at[0], ("b", 0), fdev[1])
        send(b_ref.at[pl.ds(0, half)], braw.at[1, pl.ds(0, half)], ("b", 1), fdev[2])

    def raw1():
        send(b_ref.at[pl.ds(half, half)], braw.at[1, pl.ds(half, half)], ("b", 2), fdev[2])

    def fr():
        for i in (0, 1):
            s = pl.ds(i * half, half)
            await_bytes(braw.at[1, s], ("b", 1 + i))
            send(braw.at[1, s], braw.at[2, s], ("b", 3), fdev[1])

    ex_send(0, "z", moments)
    moments = merge_moments(ex_wait(0, "z"), ROWS)
    ex_send(0, "x", moments)
    moments = merge_moments(ex_wait(0, "x"), ROWS * 2)
    ex_send(0, "y", moments)
    moments = merge_moments(ex_wait(0, "y"), ROWS * 8)
    inv = 1.0 / jnp.sqrt(moments[2:4] * (1.0 / TOTAL) + eps_norm)
    vec[0] = fold(jnp.concatenate([moments[0:2], inv], axis=0))
    for k in (1, 2, 3):
        send(vec.at[0], vec.at[k], ("v", k - 1), fdev[k])

    def normalise(src, dst, mean, iv):
        def body(i, _):
            s = pl.ds(pl.multiple_of(i * 64, 64), 64)
            dst[s, :] = ((src[s, :].astype(f32) - mean) * iv).astype(bf16)
            return 0
        lax.fori_loop(0, ROWS // 64, body, 0)

    normalise(a_ref, na, moments[0:1], inv[0:1])
    normalise(b_ref, bn.at[0], moments[1:2], inv[1:2])
    for i in range(4):
        nat[pl.ds(i * 256, 256), :] = na[pl.ds(0, ROWS), pl.ds(i * 256, 256)].T

    def d0():
        s0 = column_sum(lambda s: na[s].astype(f32) * bn[0, s].astype(f32), ROWS)
        s1 = column_sum(lambda s: na[s].astype(f32), ROWS)
        s2 = column_sum(lambda s: bn[0, s].astype(f32), ROWS)
        ex_send(1, "x", jnp.concatenate([s0, s1, s2, jnp.zeros((1, FB), f32)], axis=0))
        lacc[...] = jnp.zeros_like(lacc)
        racc[...] = jnp.zeros_like(racc)
        pay[...] = jnp.zeros_like(pay)

    def d1():
        ex_send(1, "y", unfold(total_of(ex_wait(1, "x"))))

    def d2():
        ex_send(1, "z", unfold(total_of(ex_wait(1, "y"))))

    def d3():
        sbv[0] = total_of(ex_wait(1, "z")) * (1.0 / TOTAL)
        for k in (1, 2, 3):
            send(sbv.at[0], sbv.at[k], ("f", 0), fdev[k])

    def d4():
        await_bytes(sbv.at[pl.ds(1, 3)], ("f", 0))
        rows = lax.broadcasted_iota(jnp.int32, (16, FB), 0)

        def two_terms(v):
            hi = v.astype(bf16).astype(f32)
            return jnp.where(rows == 0, hi, jnp.where(rows == 1, v - hi, 0.0)).astype(bf16)

        na[pl.ds(ROWS, 16), :] = two_terms(unfold(sbv[0])[1:2])
        for k in range(4):
            bn[k, pl.ds(ROWS, 16), :] = two_terms(unfold(sbv[k])[2:3])

    p1 = (x, y)
    p2 = (y, x)
    nb1 = ((xdev[1], xdev[3]), (ydev[1], ydev[3]))
    nb2 = (nb1[1], nb1[0])

    def at(q, d):
        return (q + d) % 4

    def piece(base, q, size, lo_, n):
        return pl.ds(pl.multiple_of(base + q * size + lo_, 16), n)

    def ring_early(buf, land, base, q, size, nb, name, c, first):
        hf = size // 2
        right, left = nb
        if first:
            send(buf.at[piece(base, at(q, 2), size, 0, hf)], land(0), (name, c, 0), right)
            send(buf.at[piece(base, at(q, 2), size, hf, hf)], land(1), (name, c, 0), left)
        else:
            send(buf.at[piece(base, at(q, 1), size, hf, hf)], land(2), (name, c, 1), right)
            send(buf.at[piece(base, at(q, 3), size, 0, hf)], land(3), (name, c, 1), left)

    def ring_late(buf, land, base, q, size, nb, name, c):
        hf = size // 2
        for m, p in ((0, piece(base, at(q, 1), size, 0, hf)),
                     (1, piece(base, at(q, 3), size, hf, hf))):
            buf[p, :] = (buf[p, :].astype(f32) + land(m)[...].astype(f32)).astype(bf16)
            send(buf.at[p], land(4 + m), (name, c, 1), nb[m])

    def ring_fin(buf, land, base, q, size, out, obase):
        hf = size // 2
        for lo_, u, v in ((0, 3, 4), (hf, 2, 5)):
            out[pl.ds(obase + lo_, hf), :] = (
                buf[piece(base, q, size, lo_, hf), :].astype(f32)
                + land(u)[...].astype(f32) + land(v)[...].astype(f32)).astype(bf16)

    def gather_early(buf, base, q, size, nb, name, c):
        own = buf.at[piece(base, q, size, 0, size)]
        for to in nb:
            send(own, own, (name, c, 0), to)

    def gather_late(buf, base, q, size, nb, name, c):
        hf = size // 2
        ha = buf.at[piece(base, at(q, 3), size, 0, hf)]
        hb = buf.at[piece(base, at(q, 1), size, hf, hf)]
        send(ha, ha, (name, c, 1), nb[0])
        send(hb, hb, (name, c, 1), nb[1])

    H = (0, 1)

    def blk(c):
        return c // CPK

    def col(c):
        return (c % CPK) * W

    def land1(c, h):
        return lambda m: ld1.at[c, (m * 2 + h)]

    def land2(c, h):
        return lambda m: ld2.at[c, (m * 2 + h)]

    def dot(c):
        k = blk(c)
        if c % CPK == 0 and k > 0:
            if k == 1:
                await_bytes(braw.at[0], ("b", 0))
            if k == 3:
                await_bytes(braw.at[2], ("b", 3))
            await_bytes(vec.at[k], ("v", k - 1))
            v = unfold(vec[k])
            normalise(braw.at[k - 1], bn.at[k], v[1:2], v[3:4])
        n = 256

        def body(j, _):
            o = pl.multiple_of(j * n, n)
            i = pl.multiple_of(col(c) + j * n, n)
            sb[c, :, pl.ds(o, n)] = jnp.dot(
                nat[...], bn[k, pl.ds(0, ROWS), pl.ds(i, n)],
                preferred_element_type=f32).astype(bf16)
            return 0

        lax.fori_loop(0, W // n, body, 0)
        for first in (True, False):
            for h in H:
                ring_early(sb.at[c], land1(c, h), 512 * h, p1[h], 128, nb1[h], "r1", c, first)

    def la(c):
        await_bytes(ld1.at[c, pl.ds(0, 4)], ("r1", c, 0))
        for h in H:
            ring_late(sb.at[c], land1(c, h), 512 * h, p1[h], 128, nb1[h], "r1", c)

    def fa(c):
        await_bytes(ld1.at[c, pl.ds(4, 8)], ("r1", c, 1))
        for h in H:
            ring_fin(sb.at[c], land1(c, h), 512 * h, p1[h], 128, sb2.at[c, h], 0)
        for first in (True, False):
            for h in H:
                ring_early(sb2.at[c, h], land2(c, h), 0, p2[h], 32, nb2[h], "r2", c, first)

    def lb(c):
        await_bytes(ld2.at[c, pl.ds(0, 4)], ("r2", c, 0))
        for h in H:
            ring_late(sb2.at[c, h], land2(c, h), 0, p2[h], 32, nb2[h], "r2", c)

    def fb(c):
        await_bytes(ld2.at[c, pl.ds(4, 8)], ("r2", c, 1))
        for h in H:
            ring_fin(sb2.at[c, h], land2(c, h), 0, p2[h], 32, ub.at[c], 32 * h)
        send(ub.at[c], zbuf.at[c], ("z", c), zhdev)

    def base2(h):
        return 512 * h + 128 * p1[h] + 32 * p2[h]

    def ti(c):
        await_bytes(zbuf.at[c], ("z", c))
        k = blk(c)
        csum = jnp.zeros((8, W), f32)
        for h in H:
            base = base2(h)
            corr = (ub[c, pl.ds(32 * h, 32), :].astype(f32)
                    + zbuf[c, pl.ds(32 * h, 32), :].astype(f32)) * (1.0 / TOTAL)
            if k == 0:
                diag = jnp.broadcast_to(unfold(sbv[0])[0:1, col(c):col(c) + W], (32, W))
                rows = base + lax.broadcasted_iota(jnp.int32, (32, W), 0)
                cols = col(c) + lax.broadcasted_iota(jnp.int32, (32, W), 1)
                on = rows == cols
                gap = 1.0 - diag
                corr = jnp.where(on, diag, corr)
                ls_ = jnp.where(on, gap * gap, lam_off * corr * corr)
                g = jnp.where(on, -2.0 * gap, 2.0 * lam_off * corr)
            else:
                ls_ = lam_off * corr * corr
                g = 2.0 * lam_off * corr
            g = g.astype(bf16)
            gt[c, pl.ds(pl.multiple_of(base, 32), 32), :] = g
            prod = g.astype(f32) * corr
            lacc[...] += jnp.sum(ls_.reshape(4, 8, W), axis=0)
            csum = csum + jnp.sum(prod.reshape(4, 8, W), axis=0)
            racc[pl.ds(32 * h, 32), :] += total_of(
                [prod[:, t * 128:(t + 1) * 128] for t in range(W // 128)])
        for h in H:
            gather_early(gt.at[c], 512 * h + 128 * p1[h], p2[h], 32, nb2[h], "g2", c)
        pay[pl.ds(2 + k, 1), pl.ds(col(c), W)] = jnp.sum(csum, axis=0, keepdims=True)

    def f2(c):
        await_bytes(gt.at[c, pl.ds(0, 128)], ("g2", c, 0))
        for h in H:
            gather_late(gt.at[c], 512 * h + 128 * p1[h], p2[h], 32, nb2[h], "g2", c)

    def g1(c):
        await_bytes(gt.at[c, pl.ds(0, 64)], ("g2", c, 1))
        for h in H:
            gather_early(gt.at[c], 512 * h, p1[h], 128, nb1[h], "g1", c)

    def f1(c):
        await_bytes(gt.at[c, pl.ds(0, 512)], ("g1", c, 0))
        for h in H:
            gather_late(gt.at[c], 512 * h, p1[h], 128, nb1[h], "g1", c)

    started = []

    def bk(c):
        await_bytes(gt.at[c, pl.ds(0, 256)], ("g1", c, 1))
        k = blk(c)
        n = 256
        cs = pl.ds(col(c), W)
        j_ = c % CPK
        first = not started
        started.append(c)

        def body_b(j, _):
            o = pl.multiple_of(j * n, n)
            i = pl.multiple_of(col(c) + j * n, n)
            v = jnp.dot(na[...], gt[c, :, pl.ds(o, n)], preferred_element_type=f32)
            if k == 0:
                acc_b[:, pl.ds(i, n)] = v
            elif k == 2:
                pbs[1, :, pl.ds(i, n)] = (
                    v + pbl[2, :, pl.ds(i, n)].astype(f32)).astype(bf16)
            else:
                pbs[k - 1, :, pl.ds(i, n)] = v.astype(bf16)
            return 0

        if k == 2:
            await_bytes(pbl.at[2, :, cs], ("p", 2, j_))
        lax.fori_loop(0, W // n, body_b, 0)
        if k != 0:
            send(pbs.at[k - 1, :, cs], pbl.at[k - 1, :, cs], ("p", k - 1, j_),
                 fdev[2] if k == 2 else fdev[1])

        def body_a(j, _):
            o = pl.multiple_of(j * n, n)
            v = lax.dot_general(bn[k, :, cs], gt[c, pl.ds(o, n), :], (((1,), (1,)), ((), ())),
                                preferred_element_type=f32)
            if first:
                acc_a[:, pl.ds(o, n)] = v
            else:
                acc_a[:, pl.ds(o, n)] += v
            return 0

        lax.fori_loop(0, FB // n, body_a, 0)

    def lo_send(base, me, to, value):
        lo[base + me] = value
        for q in to:
            send(lo.at[base + me], lo.at[base + me], ("l", base // 4), q)

    def lo_wait(base):
        await_bytes(lo.at[pl.ds(base, 3)], ("l", base // 4))
        return total_of([lo[base + q] for q in range(4)])

    def e0():
        pay[0:1, 0:W] = jnp.sum(lacc[...], axis=0, keepdims=True)
        rs = jnp.sum(racc[...], axis=1, keepdims=True)
        lanes = lax.broadcasted_iota(jnp.int32, (32, FB), 1)
        rows = lax.broadcasted_iota(jnp.int32, (32, FB), 0)
        spa = jnp.zeros((1, FB), f32)
        for h in H:
            here = lanes == base2(h) + rows
            spa = spa + jnp.sum(jnp.where(here, rs[32 * h:32 * h + 32], 0.0), axis=0, keepdims=True)
        pay[1:2, :] = spa
        lo_send(0, x, xto, pay[...])

    def e1():
        lo_send(4, y, yto, lo_wait(0))

    def e2():
        lo_send(8, fi, [fdev[1], fdev[2], fdev[3]], lo_wait(4))

    def e3():
        t = lo_wait(8)
        loss_ref[...] = jnp.full((8, 128), jnp.sum(t[0:1]), f32)

    def end():
        mine = [lo[8 + fidx[k]] for k in range(4)]
        m_a = mine[0][1:2]
        m_b = total_of([mine[k][2 + k:3 + k] for k in range(4)])
        v = unfold(vec[0])
        inv_a, inv_b = v[2:3], v[3:4]
        c_a = acc_a[ROWS:ROWS + 1, :] + acc_a[ROWS + 1:ROWS + 2, :]

        def finish_a(i, _):
            s = pl.ds(pl.multiple_of(i * 32, 32), 32)
            ga_ref[s, :] = inv_a * (acc_a[s, :] - c_a - na[s, :].astype(f32) * m_a)
            return 0

        lax.fori_loop(0, ROWS // 32, finish_a, 0)
        for j in range(CPK):
            cs = pl.ds(j * W, W)
            await_bytes(pbl.at[0, :, cs], ("p", 0, j))
            await_bytes(pbl.at[1, :, cs], ("p", 1, j))

        def back_b(s):
            return acc_b[s, :] + pbl[0, s, :].astype(f32) + pbl[1, s, :].astype(f32)

        c_b = back_b(pl.ds(ROWS, 16))
        c_b = c_b[0:1] + c_b[1:2]

        def finish_b(i, _):
            s = pl.ds(pl.multiple_of(i * 32, 32), 32)
            gb_ref[s, :] = inv_b * (back_b(s) - c_b - bn[0, s, :].astype(f32) * m_b)
            return 0

        lax.fori_loop(0, ROWS // 32, finish_b, 0)

    order = [
        (raw0,), (d0,), (dot, 0), (raw1,), (dot, 1), (la, 0), (dot, 2), (d1,), (la, 1), (dot, 3),
        (fa, 0), (la, 2), (d2,), (fa, 1), (la, 3), (fa, 2), (lb, 1), (lb, 0), (fa, 3), (lb, 2),
        (fb, 1), (fr,), (dot, 4), (fb, 2), (lb, 3), (fb, 0), (d3,), (la, 4), (dot, 6), (fa, 4), (d4,),
        (fb, 3), (la, 6), (dot, 7), (lb, 4), (fa, 6), (dot, 5), (lb, 6), (la, 7), (fb, 4), (la, 5),
        (ti, 1), (ti, 2), (fb, 6), (ti, 4), (fa, 7), (fa, 5), (ti, 6), (f2, 4), (lb, 7), (ti, 0),
        (lb, 5), (f2, 6), (g1, 4), (fb, 7), (fb, 5), (g1, 6), (f2, 0), (ti, 7), (ti, 5), (f1, 6),
        (ti, 3), (f2, 2), (f2, 1), (f2, 7), (f2, 5), (f1, 4), (e0,), (bk, 6), (g1, 7), (g1, 5),
        (f2, 3), (bk, 4), (f1, 7), (e1,), (f1, 5), (g1, 3), (g1, 2), (g1, 1), (bk, 7), (f1, 3), (e2,),
        (bk, 5), (e3,), (f1, 2), (g1, 0), (f1, 1), (bk, 3), (bk, 2), (f1, 0), (bk, 1), (bk, 0), (end,),
    ]
    for step, *args in order:
        step(*args)

    for region, name in (
        (ld1, "r1"), (ld2, "r2"), (zbuf, "z"), (gt.at[:, pl.ds(0, 192)], "g2"),
        (gt.at[:, pl.ds(0, 768)], "g1"), (braw, "b"), (vec.at[pl.ds(1, 3)], "v"),
        (sbv.at[pl.ds(1, 3)], "f"), (pbl, "p"), (ex.at[:, pl.ds(0, 7)], "e"),
        (lo.at[pl.ds(0, 9)], "l"),
    ):
        await_sent(region, name)


def shards(view_a, view_b):
    vm = pl.BlockSpec(memory_space=pltpu.VMEM)
    dma = pltpu.SemaphoreType.DMA
    scratch = [
        pltpu.VMEM((RX, FB), bf16),
        pltpu.VMEM((FB, ROWS), bf16),
        pltpu.VMEM((4, RX, FB), bf16),
        pltpu.VMEM((3, ROWS, FB), bf16),
        pltpu.VMEM((NCH, FB, W), bf16),
        pltpu.VMEM((NCH, 12, 64, W), bf16),
        pltpu.VMEM((NCH, 2, 128, W), bf16),
        pltpu.VMEM((NCH, 12, 16, W), bf16),
        pltpu.VMEM((NCH, 64, W), bf16),
        pltpu.VMEM((NCH, 64, W), bf16),
        pltpu.VMEM((NCH, FB, W), bf16),
        pltpu.VMEM((3, RX, FB), bf16),
        pltpu.VMEM((3, RX, FB), bf16),
        pltpu.VMEM((RX, FB), f32),
        pltpu.VMEM((RX, FB), f32),
        pltpu.VMEM((2, 10, 8, FB // 2), f32),
        pltpu.VMEM((12, 8, FB), f32),
        pltpu.VMEM((8, FB), f32),
        pltpu.VMEM((4, 8, FB // 2), f32),
        pltpu.VMEM((4, 8, FB // 2), f32),
        pltpu.VMEM((8, W), f32),
        pltpu.VMEM((64, 128), f32),
        dma((11,)),
        dma((NCH, 2)), dma((NCH, 2)), dma((NCH,)), dma((NCH, 2)), dma((NCH, 2)),
        dma((4,)), dma((3,)), dma((1,)), dma((3, CPK)), dma((2, 3)), dma((3,)),
    ]
    ga, gb, loss = pl.pallas_call(
        kernel,
        out_shape=(
            jax.ShapeDtypeStruct((ROWS, FB), f32),
            jax.ShapeDtypeStruct((ROWS, FB), f32),
            jax.ShapeDtypeStruct((8, 128), f32),
        ),
        in_specs=[vm, vm],
        out_specs=(vm, vm, vm),
        scratch_shapes=scratch,
        compiler_params=pltpu.CompilerParams(
            collective_id=0, has_side_effects=True, vmem_limit_bytes=60 * 2**20),
        name="barlow",
    )(view_a, view_b)
    return ga, gb, loss[0, 0]


def solution(mesh):
    return jax.shard_map(
        shards,
        mesh=mesh,
        in_specs=(P("batch", "feat"), P("batch", "feat")),
        out_specs=(P("batch", "feat"), P("batch", "feat"), P()),
        check_vma=False,
    )
```

```python
import jax
import jax.numpy as jnp
from jax import lax
from jax.experimental import pallas as pl
from jax.experimental.pallas import tpu as pltpu
from jax.sharding import PartitionSpec as P

lam_off = 0.0051
eps_norm = 1e-05
f32 = jnp.float32
bf16 = jnp.bfloat16
MESH = pl.DeviceIdType.MESH

ROWS = 512
RX = ROWS + 16
FB = 1024
CPK = 2
W = FB // CPK
NCH = 4 * CPK
TOTAL = 16384


def column_sum(fn, rows, step=32):
    def body(i, acc):
        v = fn(pl.ds(pl.multiple_of(i * step, step), step))
        return acc + jnp.sum(v.reshape(step // 8, 8, v.shape[-1]), axis=0)

    acc = lax.fori_loop(0, rows // step, body, jnp.zeros((8, FB), f32))
    return jnp.sum(acc, axis=0, keepdims=True)


def fold(v):
    w = v.shape[0] * FB // 8
    return jnp.concatenate([v[:, p * w:(p + 1) * w] for p in range(FB // w)], axis=0)


def unfold(v):
    r = v.shape[1] * 8 // FB
    return jnp.concatenate([v[p * r:(p + 1) * r] for p in range(8 // r)], axis=1)


def total_of(vs):
    t = vs[0]
    for v in vs[1:]:
        t = t + v
    return t


def kernel(
    a_ref, b_ref, ga_ref, gb_ref, loss_ref,
    na, nat, bn, braw, sb, ld1, sb2, ld2, ub, zbuf, gt, pbs, pbl, acc_a, acc_b,
    ex, ex2, mg, mb, mrow, lo, pay, vec, db, dat, dg, sbv, lacc, racc,
    ss, r1s, r2s, zs, g2s, g1s, bs, vs_, ws, fs, ps, es, e2s, ms, mbs, ls,
):
    bi = lax.axis_index("batch")
    fi = lax.axis_index("feat")
    y, zh, x = bi // 8, (bi // 4) % 2, bi % 4
    zl, core = fi // 2, fi % 2

    def dev(y_, zh_, x_, zl_, c_):
        return (((y_ + 4) % 4) * 8 + zh_ * 4 + ((x_ + 4) % 4), zl_ * 2 + c_)

    xdev = {d: dev(y, zh, x + d, zl, core) for d in (1, 2, 3)}
    ydev = {d: dev(y + d, zh, x, zl, core) for d in (1, 2, 3)}
    zhdev = dev(y, 1 - zh, x, zl, core)
    fdev = {1: dev(y, zh, x, zl, 1 - core), 2: dev(y, zh, x, 1 - zl, core),
            3: dev(y, zh, x, 1 - zl, 1 - core)}
    fidx = {0: fi, 1: zl * 2 + 1 - core, 2: (1 - zl) * 2 + core, 3: (1 - zl) * 2 + 1 - core}

    bar = pltpu.get_barrier_semaphore()
    partners = list(xdev.values()) + list(ydev.values()) + [zhdev] + list(fdev.values())
    for q in partners:
        pl.semaphore_signal(bar, inc=1, device_id=q, device_id_type=MESH)

    recv = {"r1": r1s, "r2": r2s, "z": zs, "g2": g2s, "g1": g1s, "b": bs, "v": vs_, "w": ws,
            "f": fs, "p": ps, "e": es, "d": e2s, "m": ms, "n": mbs, "l": ls}
    sent = {name: ss.at[i] for i, name in enumerate(recv)}

    def send(src, dst, key, to):
        cp = pltpu.make_async_remote_copy(
            src_ref=src, dst_ref=dst, send_sem=sent[key[0]], recv_sem=recv[key[0]].at[key[1:]],
            device_id=to, device_id_type=MESH)
        cp.start()

    def await_bytes(region, key):
        pltpu.make_async_remote_copy(
            src_ref=region, dst_ref=region, send_sem=sent[key[0]], recv_sem=recv[key[0]].at[key[1:]],
            device_id=zhdev, device_id_type=MESH).wait_recv()

    def await_sent(region, name):
        pltpu.make_async_remote_copy(
            src_ref=region, dst_ref=region, send_sem=sent[name], recv_sem=sent[name],
            device_id=zhdev, device_id_type=MESH).wait_send()

    mean_a = column_sum(lambda s: a_ref[s].astype(f32), ROWS) * (1.0 / ROWS)
    mean_b = column_sum(lambda s: b_ref[s].astype(f32), ROWS) * (1.0 / ROWS)

    mrow[0] = jnp.broadcast_to(mean_b, (8, FB))
    mb[0] = fold(mean_b)
    for i in range(4):
        s = slice(i * 256, (i + 1) * 256)
        nat[s, :] = (a_ref[:, s].astype(f32) - mean_a[:, s]).astype(bf16).T
    pl.semaphore_wait(bar, len(partners))

    xto = [xdev[d] for d in (1, 2, 3)]
    yto = [ydev[d] for d in (1, 2, 3)]
    axes = {"x": (0, 4, x, xto), "y": (4, 4, y, yto), "z": (8, 2, zh, [zhdev])}

    def ex_send(buf, name, axis, value):
        base, n, me, to = axes[axis]
        buf[base + me] = value
        for q in to:
            send(buf.at[base + me], buf.at[base + me], (name, base // 4), q)

    def ex_wait(buf, name, axis):
        base, n, me, to = axes[axis]
        await_bytes(buf.at[pl.ds(base, n - 1)], (name, base // 4))
        return total_of([buf[base + q] for q in range(n)])

    half = ROWS // 2

    def raw0():
        for k in (1, 2, 3):
            send(mb.at[0], mb.at[k], ("n", k - 1), fdev[k])
        send(b_ref, braw.at[0], ("b", 0), fdev[1])
        send(b_ref.at[pl.ds(0, half)], braw.at[1, pl.ds(0, half)], ("b", 1), fdev[2])

    def raw1():
        send(b_ref.at[pl.ds(half, half)], braw.at[1, pl.ds(half, half)], ("b", 2), fdev[2])

    def fr():
        for i in (0, 1):
            s = pl.ds(i * half, half)
            await_bytes(braw.at[1, s], ("b", 1 + i))
            send(braw.at[1, s], braw.at[2, s], ("b", 3), fdev[1])

    def group(n):
        return {1: (zh * 4 + y) * 4 + x, 4: (zh * 4 + y) * 4, 16: zh * 16}[n]

    def mg_send(n, axis):
        r = pl.ds(pl.multiple_of(group(n) * 16, 16), n * 16)
        for q in axes[axis][3]:
            send(mg.at[r], mg.at[r], ("m", axes[axis][0] // 4), q)

    def s0():
        def sums(i, acc):
            s = pl.ds(pl.multiple_of(i * 32, 32), 32)
            u = a_ref[s].astype(f32) - mean_a
            v = b_ref[s].astype(f32) - mean_b
            return tuple(t + jnp.sum(p.reshape(4, 8, FB), axis=0)
                         for t, p in zip(acc, (u * u, v * v, u * v)))

        z8 = jnp.zeros((8, FB), f32)
        acc = lax.fori_loop(0, ROWS // 32, sums, (z8, z8, z8))
        mg[pl.ds(pl.multiple_of(group(1) * 16, 16), 16), :] = jnp.concatenate(
            [m[:, p * 128:(p + 1) * 128] for p in range(8) for m in (mean_a, mean_b)], axis=0)
        mg_send(1, "x")
        ex_send(ex, "e", "x", fold(jnp.concatenate(
            [jnp.sum(t, axis=0, keepdims=True) for t in acc] + [jnp.zeros((1, FB), f32)], axis=0)))

    def s1():
        await_bytes(mg.at[pl.ds(0, 48)], ("m", 0))
        mg_send(4, "y")
        ex_send(ex, "e", "y", ex_wait(ex, "e", "x"))

    def s2():
        await_bytes(mg.at[pl.ds(0, 192)], ("m", 1))
        mg_send(16, "z")
        ex_send(ex, "e", "z", ex_wait(ex, "e", "y"))

    def s3():
        await_bytes(mg.at[pl.ds(0, 256)], ("m", 2))
        t = unfold(ex_wait(ex, "e", "z"))
        db[:, 32:128, :] = jnp.zeros((4, 96, FB), bf16)
        stat = []
        for p in range(8):
            s = slice(p * 128, (p + 1) * 128)
            da = mg[pl.ds(2 * p, 32, stride=16), :]
            dbb = mg[pl.ds(2 * p + 1, 32, stride=16), :]
            mu_a = jnp.sum(da, axis=0, keepdims=True) * (1.0 / 32)
            mu_b = jnp.sum(dbb, axis=0, keepdims=True) * (1.0 / 32)
            da = da - mu_a
            dbb = dbb - mu_b
            sq = [jnp.sum(u * v, axis=0, keepdims=True) * float(ROWS) + t[i:i + 1, s]
                  for i, (u, v) in enumerate(((da, da), (dbb, dbb), (da, dbb)))]
            inv_a = 1.0 / jnp.sqrt(sq[0] * (1.0 / TOTAL) + eps_norm)
            inv_b = 1.0 / jnp.sqrt(sq[1] * (1.0 / TOTAL) + eps_norm)
            stat.append(jnp.concatenate([mu_a, mu_b, inv_a, inv_b], axis=0))
            dg[:, s] = jnp.broadcast_to(sq[2] * (1.0 / TOTAL) * inv_a * inv_b, (8, 128))
            db[0, 0:32, s] = dbb.astype(bf16)
            dat[s, :] = jnp.concatenate([da, inv_a, jnp.zeros((95, 128), f32)], axis=0).T
        vec[0] = fold(jnp.concatenate(stat, axis=1))
        for k in (1, 2, 3):
            send(vec.at[0], vec.at[k], ("v", k - 1), fdev[k])
            send(db.at[0, pl.ds(0, 32)], db.at[k, pl.ds(0, 32)], ("w", k - 1), fdev[k])

    def normalise(src, dst, mean, iv):
        def body(i, _):
            s = pl.ds(pl.multiple_of(i * 64, 64), 64)
            dst[s, :] = ((src[s, :].astype(f32) - mean) * iv).astype(bf16)
            return 0
        lax.fori_loop(0, ROWS // 64, body, 0)

    def nm(k):
        if k > 0:
            await_bytes(vec.at[k], ("v", k - 1))
            await_bytes(db.at[k, pl.ds(0, 32)], ("w", k - 1))
        v = unfold(vec[k])
        normalise(braw.at[k - 1] if k else b_ref, bn.at[k], v[1:2], v[3:4])
        if k == 0:
            normalise(a_ref, na, v[0:1], v[2:3])

    def d0():
        s1_ = column_sum(lambda s: na[s].astype(f32), ROWS)
        s2_ = column_sum(lambda s: bn[0, s].astype(f32), ROWS)
        ex_send(ex2, "d", "x", fold(jnp.concatenate([s1_, s2_], axis=0)))

    def d1():
        ex_send(ex2, "d", "y", ex_wait(ex2, "d", "x"))

    def d2():
        ex_send(ex2, "d", "z", ex_wait(ex2, "d", "y"))

    def d3():
        sbv[0] = ex_wait(ex2, "d", "z") * (1.0 / TOTAL)
        for k in (1, 2, 3):
            send(sbv.at[0], sbv.at[k], ("f", 0), fdev[k])

    def d4():
        await_bytes(sbv.at[pl.ds(1, 3)], ("f", 0))
        rows = lax.broadcasted_iota(jnp.int32, (16, FB), 0)

        def two_terms(v):
            hi = v.astype(bf16).astype(f32)
            return jnp.where(rows == 0, hi, jnp.where(rows == 1, v - hi, 0.0)).astype(bf16)

        na[pl.ds(ROWS, 16), :] = two_terms(unfold(sbv[0])[0:1])
        for k in range(4):
            bn[k, pl.ds(ROWS, 16), :] = two_terms(unfold(sbv[k])[1:2])

    p1 = (x, y)
    p2 = (y, x)
    nb1 = ((xdev[1], xdev[3]), (ydev[1], ydev[3]))
    nb2 = (nb1[1], nb1[0])

    def at(q, d):
        return (q + d) % 4

    def piece(base, q, size, lo_, n):
        return pl.ds(pl.multiple_of(base + q * size + lo_, 16), n)

    def ring_early(buf, land, base, q, size, nb, name, c, first):
        hf = size // 2
        right, left = nb
        if first:
            send(buf.at[piece(base, at(q, 2), size, 0, hf)], land(0), (name, c, 0), right)
            send(buf.at[piece(base, at(q, 2), size, hf, hf)], land(1), (name, c, 0), left)
        else:
            send(buf.at[piece(base, at(q, 1), size, hf, hf)], land(2), (name, c, 1), right)
            send(buf.at[piece(base, at(q, 3), size, 0, hf)], land(3), (name, c, 1), left)

    def ring_late(buf, land, base, q, size, nb, name, c):
        hf = size // 2
        for m, p in ((0, piece(base, at(q, 1), size, 0, hf)),
                     (1, piece(base, at(q, 3), size, hf, hf))):
            buf[p, :] = (buf[p, :].astype(f32) + land(m)[...].astype(f32)).astype(bf16)
            send(buf.at[p], land(4 + m), (name, c, 1), nb[m])

    def ring_fin(buf, land, base, q, size, out, obase):
        hf = size // 2
        for lo_, u, v in ((0, 3, 4), (hf, 2, 5)):
            out[pl.ds(obase + lo_, hf), :] = (
                buf[piece(base, q, size, lo_, hf), :].astype(f32)
                + land(u)[...].astype(f32) + land(v)[...].astype(f32)).astype(bf16)

    def gather_early(buf, base, q, size, nb, name, c):
        own = buf.at[piece(base, q, size, 0, size)]
        for to in nb:
            send(own, own, (name, c, 0), to)

    def gather_late(buf, base, q, size, nb, name, c):
        hf = size // 2
        ha = buf.at[piece(base, at(q, 3), size, 0, hf)]
        hb = buf.at[piece(base, at(q, 1), size, hf, hf)]
        send(ha, ha, (name, c, 1), nb[0])
        send(hb, hb, (name, c, 1), nb[1])

    H = (0, 1)

    def blk(c):
        return c // CPK

    def col(c):
        return (c % CPK) * W

    def land1(c, h):
        return lambda m: ld1.at[c, (m * 2 + h)]

    def land2(c, h):
        return lambda m: ld2.at[c, (m * 2 + h)]

    def dot(c):
        k = blk(c)
        src = b_ref if k == 0 else braw.at[k - 1]
        if c % CPK == 0 and k > 0:
            if k == 1:
                await_bytes(braw.at[0], ("b", 0))
            if k == 3:
                await_bytes(braw.at[2], ("b", 3))
            await_bytes(mb.at[k], ("n", k - 1))
            mrow[k] = jnp.broadcast_to(unfold(mb[k]), (8, FB))
        n = 256

        def body(j, _):
            o = pl.multiple_of(j * n, n)
            i = pl.multiple_of(col(c) + j * n, n)
            centered = (src[:, pl.ds(i, n)].astype(f32) - mrow[k, 0:1, pl.ds(i, n)]).astype(bf16)
            sb[c, :, pl.ds(o, n)] = jnp.dot(
                nat[...], centered, preferred_element_type=f32).astype(bf16)
            return 0

        lax.fori_loop(0, W // n, body, 0)
        for first in (True, False):
            for h in H:
                ring_early(sb.at[c], land1(c, h), 512 * h, p1[h], 128, nb1[h], "r1", c, first)

    def la(c):
        await_bytes(ld1.at[c, pl.ds(0, 4)], ("r1", c, 0))
        for h in H:
            ring_late(sb.at[c], land1(c, h), 512 * h, p1[h], 128, nb1[h], "r1", c)

    def fa(c):
        await_bytes(ld1.at[c, pl.ds(4, 8)], ("r1", c, 1))
        for h in H:
            ring_fin(sb.at[c], land1(c, h), 512 * h, p1[h], 128, sb2.at[c, h], 0)
        for first in (True, False):
            for h in H:
                ring_early(sb2.at[c, h], land2(c, h), 0, p2[h], 32, nb2[h], "r2", c, first)

    def lb(c):
        await_bytes(ld2.at[c, pl.ds(0, 4)], ("r2", c, 0))
        for h in H:
            ring_late(sb2.at[c, h], land2(c, h), 0, p2[h], 32, nb2[h], "r2", c)

    def fb(c):
        await_bytes(ld2.at[c, pl.ds(4, 8)], ("r2", c, 1))
        for h in H:
            ring_fin(sb2.at[c, h], land2(c, h), 0, p2[h], 32, ub.at[c], 32 * h)
        send(ub.at[c], zbuf.at[c], ("z", c), zhdev)

    def base2(h):
        return 512 * h + 128 * p1[h] + 32 * p2[h]

    def ti(c):
        await_bytes(zbuf.at[c], ("z", c))
        k = blk(c)
        csum = jnp.zeros((8, W), f32)
        inv_b = unfold(vec[k])[3:4, col(c):col(c) + W]
        for h in H:
            base = base2(h)
            mine = dat[pl.ds(pl.multiple_of(base, 32), 32), :]
            corr = (ub[c, pl.ds(32 * h, 32), :].astype(f32)
                    + zbuf[c, pl.ds(32 * h, 32), :].astype(f32)
                    + float(ROWS) * jnp.dot(mine.astype(bf16), db[k, :, col(c):col(c) + W],
                                            preferred_element_type=f32))
            corr = corr * (mine[:, 32:33] * (1.0 / TOTAL)) * inv_b
            if k == 0:
                diag = jnp.broadcast_to(dg[0:1, col(c):col(c) + W], (32, W))
                rows = base + lax.broadcasted_iota(jnp.int32, (32, W), 0)
                cols = col(c) + lax.broadcasted_iota(jnp.int32, (32, W), 1)
                on = rows == cols
                gap = 1.0 - diag
                corr = jnp.where(on, diag, corr)
                ls_ = jnp.where(on, gap * gap, lam_off * corr * corr)
                g = jnp.where(on, -2.0 * gap, 2.0 * lam_off * corr)
            else:
                ls_ = lam_off * corr * corr
                g = 2.0 * lam_off * corr
            g = g.astype(bf16)
            gt[c, pl.ds(pl.multiple_of(base, 32), 32), :] = g
            prod = g.astype(f32) * corr
            lacc[...] += jnp.sum(ls_.reshape(4, 8, W), axis=0)
            csum = csum + jnp.sum(prod.reshape(4, 8, W), axis=0)
            racc[pl.ds(32 * h, 32), :] += total_of(
                [prod[:, t * 128:(t + 1) * 128] for t in range(W // 128)])
        for h in H:
            gather_early(gt.at[c], 512 * h + 128 * p1[h], p2[h], 32, nb2[h], "g2", c)
        pay[pl.ds(2 + k, 1), pl.ds(col(c), W)] = jnp.sum(csum, axis=0, keepdims=True)

    def f2(c):
        await_bytes(gt.at[c, pl.ds(0, 128)], ("g2", c, 0))
        for h in H:
            gather_late(gt.at[c], 512 * h + 128 * p1[h], p2[h], 32, nb2[h], "g2", c)

    def g1(c):
        await_bytes(gt.at[c, pl.ds(0, 64)], ("g2", c, 1))
        for h in H:
            gather_early(gt.at[c], 512 * h, p1[h], 128, nb1[h], "g1", c)

    def f1(c):
        await_bytes(gt.at[c, pl.ds(0, 512)], ("g1", c, 0))
        for h in H:
            gather_late(gt.at[c], 512 * h, p1[h], 128, nb1[h], "g1", c)

    started = []

    def bk(c):
        await_bytes(gt.at[c, pl.ds(0, 256)], ("g1", c, 1))
        k = blk(c)
        n = 256
        cs = pl.ds(col(c), W)
        j_ = c % CPK
        first = not started
        started.append(c)

        def body_b(j, _):
            o = pl.multiple_of(j * n, n)
            i = pl.multiple_of(col(c) + j * n, n)
            v = jnp.dot(na[...], gt[c, :, pl.ds(o, n)], preferred_element_type=f32)
            if k == 0:
                acc_b[:, pl.ds(i, n)] = v
            elif k == 2:
                pbs[1, :, pl.ds(i, n)] = (
                    v + pbl[2, :, pl.ds(i, n)].astype(f32)).astype(bf16)
            else:
                pbs[k - 1, :, pl.ds(i, n)] = v.astype(bf16)
            return 0

        if k == 2:
            await_bytes(pbl.at[2, :, cs], ("p", 2, j_))
        lax.fori_loop(0, W // n, body_b, 0)
        if k != 0:
            send(pbs.at[k - 1, :, cs], pbl.at[k - 1, :, cs], ("p", k - 1, j_),
                 fdev[2] if k == 2 else fdev[1])

        def body_a(j, _):
            o = pl.multiple_of(j * n, n)
            v = lax.dot_general(bn[k, :, cs], gt[c, pl.ds(o, n), :], (((1,), (1,)), ((), ())),
                                preferred_element_type=f32)
            if first:
                acc_a[:, pl.ds(o, n)] = v
            else:
                acc_a[:, pl.ds(o, n)] += v
            return 0

        lax.fori_loop(0, FB // n, body_a, 0)

    def lo_send(base, me, to, value):
        lo[base + me] = value
        for q in to:
            send(lo.at[base + me], lo.at[base + me], ("l", base // 4), q)

    def lo_wait(base):
        await_bytes(lo.at[pl.ds(base, 3)], ("l", base // 4))
        return total_of([lo[base + q] for q in range(4)])

    def e0():
        pay[0:1, 0:W] = jnp.sum(lacc[...], axis=0, keepdims=True)
        rs = jnp.sum(racc[...], axis=1, keepdims=True)
        lanes = lax.broadcasted_iota(jnp.int32, (32, FB), 1)
        rows = lax.broadcasted_iota(jnp.int32, (32, FB), 0)
        spa = jnp.zeros((1, FB), f32)
        for h in H:
            here = lanes == base2(h) + rows
            spa = spa + jnp.sum(jnp.where(here, rs[32 * h:32 * h + 32], 0.0), axis=0, keepdims=True)
        pay[1:2, :] = spa
        lo_send(0, x, xto, pay[...])

    def e1():
        lo_send(4, y, yto, lo_wait(0))

    def e2():
        lo_send(8, fi, [fdev[1], fdev[2], fdev[3]], lo_wait(4))

    def e3():
        t = lo_wait(8)
        loss_ref[...] = jnp.full((8, 128), jnp.sum(t[0:1]), f32)

    def end():
        mine = [lo[8 + fidx[k]] for k in range(4)]
        m_a = mine[0][1:2]
        m_b = total_of([mine[k][2 + k:3 + k] for k in range(4)])
        v = unfold(vec[0])
        inv_a, inv_b = v[2:3], v[3:4]
        c_a = acc_a[ROWS:ROWS + 1, :] + acc_a[ROWS + 1:ROWS + 2, :]

        def finish_a(i, _):
            s = pl.ds(pl.multiple_of(i * 32, 32), 32)
            ga_ref[s, :] = inv_a * (acc_a[s, :] - c_a - na[s, :].astype(f32) * m_a)
            return 0

        lax.fori_loop(0, ROWS // 32, finish_a, 0)
        for j in range(CPK):
            cs = pl.ds(j * W, W)
            await_bytes(pbl.at[0, :, cs], ("p", 0, j))
            await_bytes(pbl.at[1, :, cs], ("p", 1, j))

        def back_b(s):
            return acc_b[s, :] + pbl[0, s, :].astype(f32) + pbl[1, s, :].astype(f32)

        c_b = back_b(pl.ds(ROWS, 16))
        c_b = c_b[0:1] + c_b[1:2]

        def finish_b(i, _):
            s = pl.ds(pl.multiple_of(i * 32, 32), 32)
            gb_ref[s, :] = inv_b * (back_b(s) - c_b - bn[0, s, :].astype(f32) * m_b)
            return 0

        lax.fori_loop(0, ROWS // 32, finish_b, 0)

    lacc[...] = jnp.zeros_like(lacc)
    racc[...] = jnp.zeros_like(racc)
    pay[...] = jnp.zeros_like(pay)

    order = [
        (raw0,), (raw1,), (dot, 0), (s0,), (dot, 1), (dot, 2), (s1,), (la, 0), (dot, 3), (la, 1),
        (la, 2), (fa, 0), (s2,), (la, 3), (fa, 2), (lb, 0), (fa, 1), (fa, 3), (lb, 2), (fr,), (dot, 4),
        (fb, 0), (lb, 1), (lb, 3), (fb, 2), (la, 4), (dot, 6), (s3,), (fa, 4), (la, 6), (dot, 5),
        (fb, 1), (lb, 4), (nm, 1), (fb, 3), (fa, 6), (dot, 7), (nm, 0), (fb, 4), (lb, 6), (la, 5),
        (d0,), (nm, 3), (la, 7), (ti, 3), (fb, 6), (nm, 2), (ti, 4), (fa, 5), (ti, 0), (d1,), (fa, 7),
        (ti, 6), (lb, 5), (f2, 4), (ti, 1), (ti, 2), (d2,), (lb, 7), (f2, 6), (g1, 4), (fb, 5),
        (fb, 7), (g1, 6), (f2, 2), (d3,), (ti, 5), (f2, 0), (ti, 7), (d4,), (f1, 6), (e0,), (f1, 4),
        (f2, 7), (f2, 5), (g1, 0), (bk, 6), (e1,), (g1, 7), (g1, 5), (bk, 4), (e2,), (f1, 7), (f2, 1),
        (f2, 3), (g1, 2), (f1, 5), (f1, 0), (bk, 7), (g1, 3), (g1, 1), (f1, 2), (bk, 5), (f1, 3),
        (e3,), (bk, 0), (f1, 1), (bk, 2), (bk, 3), (bk, 1), (end,),
    ]
    for step, *args in order:
        step(*args)

    for region, name in (
        (mg.at[pl.ds(0, 48 + 192 + 256)], "m"), (mb.at[pl.ds(1, 3)], "n"),
        (db.at[pl.ds(1, 3), pl.ds(0, 32)], "w"), (ex2.at[pl.ds(0, 7)], "d"),
        (ld1, "r1"), (ld2, "r2"), (zbuf, "z"), (gt.at[:, pl.ds(0, 192)], "g2"),
        (gt.at[:, pl.ds(0, 768)], "g1"), (braw, "b"), (vec.at[pl.ds(1, 3)], "v"),
        (sbv.at[pl.ds(1, 3)], "f"), (pbl, "p"), (ex.at[pl.ds(0, 7)], "e"),
        (lo.at[pl.ds(0, 9)], "l"),
    ):
        await_sent(region, name)


def shards(view_a, view_b):
    vm = pl.BlockSpec(memory_space=pltpu.VMEM)
    dma = pltpu.SemaphoreType.DMA
    scratch = [
        pltpu.VMEM((RX, FB), bf16),
        pltpu.VMEM((FB, ROWS), bf16),
        pltpu.VMEM((4, RX, FB), bf16),
        pltpu.VMEM((3, ROWS, FB), bf16),
        pltpu.VMEM((NCH, FB, W), bf16),
        pltpu.VMEM((NCH, 12, 64, W), bf16),
        pltpu.VMEM((NCH, 2, 128, W), bf16),
        pltpu.VMEM((NCH, 12, 16, W), bf16),
        pltpu.VMEM((NCH, 64, W), bf16),
        pltpu.VMEM((NCH, 64, W), bf16),
        pltpu.VMEM((NCH, FB, W), bf16),
        pltpu.VMEM((3, RX, FB), bf16),
        pltpu.VMEM((3, RX, FB), bf16),
        pltpu.VMEM((RX, FB), f32),
        pltpu.VMEM((RX, FB), f32),
        pltpu.VMEM((10, 8, FB // 2), f32),
        pltpu.VMEM((10, 8, FB // 4), f32),
        pltpu.VMEM((32 * 16, 128), f32),
        pltpu.VMEM((4, 8, FB // 8), f32),
        pltpu.VMEM((4, 8, FB), f32),
        pltpu.VMEM((12, 8, FB), f32),
        pltpu.VMEM((8, FB), f32),
        pltpu.VMEM((4, 8, FB // 2), f32),
        pltpu.VMEM((4, 128, FB), bf16),
        pltpu.VMEM((FB, 128), f32),
        pltpu.VMEM((8, FB), f32),
        pltpu.VMEM((4, 8, FB // 4), f32),
        pltpu.VMEM((8, W), f32),
        pltpu.VMEM((64, 128), f32),
        dma((15,)),
        dma((NCH, 2)), dma((NCH, 2)), dma((NCH,)), dma((NCH, 2)), dma((NCH, 2)),
        dma((4,)), dma((3,)), dma((3,)), dma((1,)), dma((3, CPK)), dma((3,)), dma((3,)), dma((3,)),
        dma((3,)), dma((3,)),
    ]
    ga, gb, loss = pl.pallas_call(
        kernel,
        out_shape=(
            jax.ShapeDtypeStruct((ROWS, FB), f32),
            jax.ShapeDtypeStruct((ROWS, FB), f32),
            jax.ShapeDtypeStruct((8, 128), f32),
        ),
        in_specs=[vm, vm],
        out_specs=(vm, vm, vm),
        scratch_shapes=scratch,
        compiler_params=pltpu.CompilerParams(
            collective_id=0, has_side_effects=True, vmem_limit_bytes=60 * 2**20),
        name="barlow",
    )(view_a, view_b)
    return ga, gb, loss[0, 0]


def solution(mesh):
    return jax.shard_map(
        shards,
        mesh=mesh,
        in_specs=(P("batch", "feat"), P("batch", "feat")),
        out_specs=(P("batch", "feat"), P("batch", "feat"), P()),
        check_vma=False,
    )
```

```python
import jax
import jax.numpy as jnp
from jax import lax
from jax.experimental import pallas as pl
from jax.experimental.pallas import tpu as pltpu
from jax.sharding import PartitionSpec as P

lam_off = 0.0051
eps_norm = 1e-05
f32 = jnp.float32
bf16 = jnp.bfloat16
MESH = pl.DeviceIdType.MESH

ROWS = 512
RX = ROWS + 16
FB = 1024
CPK = 2
W = FB // CPK
NCH = 4 * CPK
TOTAL = 16384


def column_sum(fn, rows, step=32):
    def body(i, acc):
        v = fn(pl.ds(pl.multiple_of(i * step, step), step))
        return acc + jnp.sum(v.reshape(step // 8, 8, v.shape[-1]), axis=0)

    acc = lax.fori_loop(0, rows // step, body, jnp.zeros((8, FB), f32))
    return jnp.sum(acc, axis=0, keepdims=True)


def fold(v):
    w = v.shape[0] * FB // 8
    return jnp.concatenate([v[:, p * w:(p + 1) * w] for p in range(FB // w)], axis=0)


def unfold(v):
    r = v.shape[1] * 8 // FB
    return jnp.concatenate([v[p * r:(p + 1) * r] for p in range(8 // r)], axis=1)


def total_of(vs):
    t = vs[0]
    for v in vs[1:]:
        t = t + v
    return t


def kernel(
    a_ref, b_ref, ga_ref, gb_ref, loss_ref,
    na, nat, bn, braw, sb, ld1, sb2, ld2, ub, zbuf, gt, pbs, pbl, acc_a, acc_b,
    ex, ex2, mg, mb, mrow, lo, pay, vec, db, dat, dg, sbv, lacc, racc,
    ss, r1s, r2s, zs, g2s, g1s, bs, vs_, ws, fs, ps, es, e2s, ms, mbs, ls,
):
    bi = lax.axis_index("batch")
    fi = lax.axis_index("feat")
    y, zh, x = bi // 8, (bi // 4) % 2, bi % 4
    zl, core = fi // 2, fi % 2

    def dev(y_, zh_, x_, zl_, c_):
        return (((y_ + 4) % 4) * 8 + zh_ * 4 + ((x_ + 4) % 4), zl_ * 2 + c_)

    xdev = {d: dev(y, zh, x + d, zl, core) for d in (1, 2, 3)}
    ydev = {d: dev(y + d, zh, x, zl, core) for d in (1, 2, 3)}
    zhdev = dev(y, 1 - zh, x, zl, core)
    fdev = {1: dev(y, zh, x, zl, 1 - core), 2: dev(y, zh, x, 1 - zl, core),
            3: dev(y, zh, x, 1 - zl, 1 - core)}
    fidx = {0: fi, 1: zl * 2 + 1 - core, 2: (1 - zl) * 2 + core, 3: (1 - zl) * 2 + 1 - core}

    bar = pltpu.get_barrier_semaphore()
    partners = list(xdev.values()) + list(ydev.values()) + [zhdev] + list(fdev.values())
    for q in partners:
        pl.semaphore_signal(bar, inc=1, device_id=q, device_id_type=MESH)

    recv = {"r1": r1s, "r2": r2s, "z": zs, "g2": g2s, "g1": g1s, "b": bs, "v": vs_, "w": ws,
            "f": fs, "p": ps, "e": es, "d": e2s, "m": ms, "n": mbs, "l": ls}
    sent = {name: ss.at[i] for i, name in enumerate(recv)}

    def send(src, dst, key, to):
        cp = pltpu.make_async_remote_copy(
            src_ref=src, dst_ref=dst, send_sem=sent[key[0]], recv_sem=recv[key[0]].at[key[1:]],
            device_id=to, device_id_type=MESH)
        cp.start()

    def await_bytes(region, key):
        pltpu.make_async_remote_copy(
            src_ref=region, dst_ref=region, send_sem=sent[key[0]], recv_sem=recv[key[0]].at[key[1:]],
            device_id=zhdev, device_id_type=MESH).wait_recv()

    def await_sent(region, name):
        pltpu.make_async_remote_copy(
            src_ref=region, dst_ref=region, send_sem=sent[name], recv_sem=sent[name],
            device_id=zhdev, device_id_type=MESH).wait_send()

    def multiply(c, src):
        k = c // CPK
        o = c % CPK * W
        centered = (src[:, o:o + W].astype(f32) - mrow[k, 0:1, o:o + W]).astype(bf16)
        sb[c] = jnp.dot(nat[...], centered, preferred_element_type=f32).astype(bf16)

    mean_a = column_sum(lambda s: a_ref[s].astype(f32), ROWS) * (1.0 / ROWS)
    mean_b = column_sum(lambda s: b_ref[s].astype(f32), ROWS) * (1.0 / ROWS)

    mrow[0] = jnp.broadcast_to(mean_b, (8, FB))
    mb[0] = fold(mean_b)
    for i in range(4):
        s = slice(i * 256, (i + 1) * 256)
        nat[s, :] = (a_ref[:, s].astype(f32) - mean_a[:, s]).astype(bf16).T
    multiply(0, b_ref)

    def local_sums(i, acc):
        s = pl.ds(pl.multiple_of(i * 32, 32), 32)
        u = a_ref[s].astype(f32) - mean_a
        v = b_ref[s].astype(f32) - mean_b
        return tuple(t + jnp.sum(p.reshape(4, 8, FB), axis=0)
                     for t, p in zip(acc, (u * u, v * v, u * v)))

    z8 = jnp.zeros((8, FB), f32)
    local = [jnp.sum(t, axis=0, keepdims=True)
             for t in lax.fori_loop(0, ROWS // 32, local_sums, (z8, z8, z8))]
    lacc[...] = jnp.zeros_like(lacc)
    racc[...] = jnp.zeros_like(racc)
    pay[...] = jnp.zeros_like(pay)
    pl.semaphore_wait(bar, len(partners))

    xto = [xdev[d] for d in (1, 2, 3)]
    yto = [ydev[d] for d in (1, 2, 3)]
    axes = {"x": (0, 4, x, xto), "y": (4, 4, y, yto), "z": (8, 2, zh, [zhdev])}

    def ex_send(buf, name, axis, value):
        base, n, me, to = axes[axis]
        buf[base + me] = value
        for q in to:
            send(buf.at[base + me], buf.at[base + me], (name, base // 4), q)

    def ex_wait(buf, name, axis):
        base, n, me, to = axes[axis]
        await_bytes(buf.at[pl.ds(base, n - 1)], (name, base // 4))
        return total_of([buf[base + q] for q in range(n)])

    half = ROWS // 2

    def raw0():
        for k in (1, 2, 3):
            send(mb.at[0], mb.at[k], ("n", k - 1), fdev[k])
        send(b_ref, braw.at[0], ("b", 0), fdev[1])
        send(b_ref.at[pl.ds(0, half)], braw.at[1, pl.ds(0, half)], ("b", 1), fdev[2])

    def raw1():
        send(b_ref.at[pl.ds(half, half)], braw.at[1, pl.ds(half, half)], ("b", 2), fdev[2])

    def fr():
        for i in (0, 1):
            s = pl.ds(i * half, half)
            await_bytes(braw.at[1, s], ("b", 1 + i))
            send(braw.at[1, s], braw.at[2, s], ("b", 3), fdev[1])

    def group(n):
        return {1: (zh * 4 + y) * 4 + x, 4: (zh * 4 + y) * 4, 16: zh * 16}[n]

    def mg_send(n, axis):
        r = pl.ds(pl.multiple_of(group(n) * 16, 16), n * 16)
        for q in axes[axis][3]:
            send(mg.at[r], mg.at[r], ("m", axes[axis][0] // 4), q)

    def s0():
        mg[pl.ds(pl.multiple_of(group(1) * 16, 16), 16), :] = jnp.concatenate(
            [m[:, p * 128:(p + 1) * 128] for p in range(8) for m in (mean_a, mean_b)], axis=0)
        mg_send(1, "x")
        ex_send(ex, "e", "x", fold(jnp.concatenate(
            local + [jnp.zeros((1, FB), f32)], axis=0)))

    def s1():
        await_bytes(mg.at[pl.ds(0, 48)], ("m", 0))
        mg_send(4, "y")
        ex_send(ex, "e", "y", ex_wait(ex, "e", "x"))

    def s2():
        await_bytes(mg.at[pl.ds(0, 192)], ("m", 1))
        mg_send(16, "z")
        ex_send(ex, "e", "z", ex_wait(ex, "e", "y"))

    def s3():
        await_bytes(mg.at[pl.ds(0, 256)], ("m", 2))
        t = unfold(ex_wait(ex, "e", "z"))
        db[:, 32:128, :] = jnp.zeros((4, 96, FB), bf16)
        stat = []
        for p in range(8):
            s = slice(p * 128, (p + 1) * 128)
            da = mg[pl.ds(2 * p, 32, stride=16), :]
            dbb = mg[pl.ds(2 * p + 1, 32, stride=16), :]
            mu_a = jnp.sum(da, axis=0, keepdims=True) * (1.0 / 32)
            mu_b = jnp.sum(dbb, axis=0, keepdims=True) * (1.0 / 32)
            da = da - mu_a
            dbb = dbb - mu_b
            sq = [jnp.sum(u * v, axis=0, keepdims=True) * float(ROWS) + t[i:i + 1, s]
                  for i, (u, v) in enumerate(((da, da), (dbb, dbb), (da, dbb)))]
            inv_a = 1.0 / jnp.sqrt(sq[0] * (1.0 / TOTAL) + eps_norm)
            inv_b = 1.0 / jnp.sqrt(sq[1] * (1.0 / TOTAL) + eps_norm)
            stat.append(jnp.concatenate([mu_a, mu_b, inv_a, inv_b], axis=0))
            dg[:, s] = jnp.broadcast_to(sq[2] * (1.0 / TOTAL) * inv_a * inv_b, (8, 128))
            db[0, 0:32, s] = dbb.astype(bf16)
            dat[s, :] = jnp.concatenate([da, inv_a, jnp.zeros((95, 128), f32)], axis=0).T
        vec[0] = fold(jnp.concatenate(stat, axis=1))
        for k in (1, 2, 3):
            send(vec.at[0], vec.at[k], ("v", k - 1), fdev[k])
            send(db.at[0, pl.ds(0, 32)], db.at[k, pl.ds(0, 32)], ("w", k - 1), fdev[k])

    def normalise(src, dst, mean, iv):
        def body(i, _):
            s = pl.ds(pl.multiple_of(i * 64, 64), 64)
            dst[s, :] = ((src[s, :].astype(f32) - mean) * iv).astype(bf16)
            return 0
        lax.fori_loop(0, ROWS // 64, body, 0)

    def nm(k):
        if k > 0:
            await_bytes(vec.at[k], ("v", k - 1))
            await_bytes(db.at[k, pl.ds(0, 32)], ("w", k - 1))
        v = unfold(vec[k])
        normalise(braw.at[k - 1] if k else b_ref, bn.at[k], v[1:2], v[3:4])
        if k == 0:
            normalise(a_ref, na, v[0:1], v[2:3])

    def d0():
        s1_ = column_sum(lambda s: na[s].astype(f32), ROWS)
        s2_ = column_sum(lambda s: bn[0, s].astype(f32), ROWS)
        ex_send(ex2, "d", "x", fold(jnp.concatenate([s1_, s2_], axis=0)))

    def d1():
        ex_send(ex2, "d", "y", ex_wait(ex2, "d", "x"))

    def d2():
        ex_send(ex2, "d", "z", ex_wait(ex2, "d", "y"))

    def d3():
        sbv[0] = ex_wait(ex2, "d", "z") * (1.0 / TOTAL)
        for k in (1, 2, 3):
            send(sbv.at[0], sbv.at[k], ("f", 0), fdev[k])

    def d4():
        await_bytes(sbv.at[pl.ds(1, 3)], ("f", 0))
        rows = lax.broadcasted_iota(jnp.int32, (16, FB), 0)

        def two_terms(v):
            hi = v.astype(bf16).astype(f32)
            return jnp.where(rows == 0, hi, jnp.where(rows == 1, v - hi, 0.0)).astype(bf16)

        na[pl.ds(ROWS, 16), :] = two_terms(unfold(sbv[0])[0:1])
        for k in range(4):
            bn[k, pl.ds(ROWS, 16), :] = two_terms(unfold(sbv[k])[1:2])

    p1 = (x, y)
    p2 = (y, x)
    nb1 = ((xdev[1], xdev[3]), (ydev[1], ydev[3]))
    nb2 = (nb1[1], nb1[0])

    def at(q, d):
        return (q + d) % 4

    def piece(base, q, size, lo_, n):
        return pl.ds(pl.multiple_of(base + q * size + lo_, 16), n)

    def ring_early(buf, land, base, q, size, nb, name, c, first):
        hf = size // 2
        right, left = nb
        if first:
            send(buf.at[piece(base, at(q, 2), size, 0, hf)], land(0), (name, c, 0), right)
            send(buf.at[piece(base, at(q, 2), size, hf, hf)], land(1), (name, c, 0), left)
        else:
            send(buf.at[piece(base, at(q, 1), size, hf, hf)], land(2), (name, c, 1), right)
            send(buf.at[piece(base, at(q, 3), size, 0, hf)], land(3), (name, c, 1), left)

    def ring_late(buf, land, base, q, size, nb, name, c):
        hf = size // 2
        for m, p in ((0, piece(base, at(q, 1), size, 0, hf)),
                     (1, piece(base, at(q, 3), size, hf, hf))):
            buf[p, :] = (buf[p, :].astype(f32) + land(m)[...].astype(f32)).astype(bf16)
            send(buf.at[p], land(4 + m), (name, c, 1), nb[m])

    def ring_fin(buf, land, base, q, size, out, obase):
        hf = size // 2
        for lo_, u, v in ((0, 3, 4), (hf, 2, 5)):
            out[pl.ds(obase + lo_, hf), :] = (
                buf[piece(base, q, size, lo_, hf), :].astype(f32)
                + land(u)[...].astype(f32) + land(v)[...].astype(f32)).astype(bf16)

    def gather_early(buf, base, q, size, nb, name, c):
        own = buf.at[piece(base, q, size, 0, size)]
        for to in nb:
            send(own, own, (name, c, 0), to)

    def gather_late(buf, base, q, size, nb, name, c):
        hf = size // 2
        ha = buf.at[piece(base, at(q, 3), size, 0, hf)]
        hb = buf.at[piece(base, at(q, 1), size, hf, hf)]
        send(ha, ha, (name, c, 1), nb[0])
        send(hb, hb, (name, c, 1), nb[1])

    H = (0, 1)

    def blk(c):
        return c // CPK

    def col(c):
        return (c % CPK) * W

    def land1(c, h):
        return lambda m: ld1.at[c, (m * 2 + h)]

    def land2(c, h):
        return lambda m: ld2.at[c, (m * 2 + h)]

    def dot(c):
        k = blk(c)
        src = b_ref if k == 0 else braw.at[k - 1]
        if c % CPK == 0 and k > 0:
            if k == 1:
                await_bytes(braw.at[0], ("b", 0))
            if k == 3:
                await_bytes(braw.at[2], ("b", 3))
            await_bytes(mb.at[k], ("n", k - 1))
            mrow[k] = jnp.broadcast_to(unfold(mb[k]), (8, FB))
        if c > 0:
            multiply(c, src)
        for first in (True, False):
            for h in H:
                ring_early(sb.at[c], land1(c, h), 512 * h, p1[h], 128, nb1[h], "r1", c, first)

    def la(c):
        await_bytes(ld1.at[c, pl.ds(0, 4)], ("r1", c, 0))
        for h in H:
            ring_late(sb.at[c], land1(c, h), 512 * h, p1[h], 128, nb1[h], "r1", c)

    def fa(c):
        await_bytes(ld1.at[c, pl.ds(4, 8)], ("r1", c, 1))
        for h in H:
            ring_fin(sb.at[c], land1(c, h), 512 * h, p1[h], 128, sb2.at[c, h], 0)
        for first in (True, False):
            for h in H:
                ring_early(sb2.at[c, h], land2(c, h), 0, p2[h], 32, nb2[h], "r2", c, first)

    def lb(c):
        await_bytes(ld2.at[c, pl.ds(0, 4)], ("r2", c, 0))
        for h in H:
            ring_late(sb2.at[c, h], land2(c, h), 0, p2[h], 32, nb2[h], "r2", c)

    def fb(c):
        await_bytes(ld2.at[c, pl.ds(4, 8)], ("r2", c, 1))
        for h in H:
            ring_fin(sb2.at[c, h], land2(c, h), 0, p2[h], 32, ub.at[c], 32 * h)
        send(ub.at[c], zbuf.at[c], ("z", c), zhdev)

    def base2(h):
        return 512 * h + 128 * p1[h] + 32 * p2[h]

    def ti(c):
        await_bytes(zbuf.at[c], ("z", c))
        k = blk(c)
        csum = jnp.zeros((8, W), f32)
        inv_b = unfold(vec[k])[3:4, col(c):col(c) + W]
        for h in H:
            base = base2(h)
            mine = dat[pl.ds(pl.multiple_of(base, 32), 32), :]
            corr = (ub[c, pl.ds(32 * h, 32), :].astype(f32)
                    + zbuf[c, pl.ds(32 * h, 32), :].astype(f32)
                    + float(ROWS) * jnp.dot(mine.astype(bf16), db[k, :, col(c):col(c) + W],
                                            preferred_element_type=f32))
            corr = corr * (mine[:, 32:33] * (1.0 / TOTAL)) * inv_b
            if k == 0:
                diag = jnp.broadcast_to(dg[0:1, col(c):col(c) + W], (32, W))
                rows = base + lax.broadcasted_iota(jnp.int32, (32, W), 0)
                cols = col(c) + lax.broadcasted_iota(jnp.int32, (32, W), 1)
                on = rows == cols
                gap = 1.0 - diag
                corr = jnp.where(on, diag, corr)
                ls_ = jnp.where(on, gap * gap, lam_off * corr * corr)
                g = jnp.where(on, -2.0 * gap, 2.0 * lam_off * corr)
            else:
                ls_ = lam_off * corr * corr
                g = 2.0 * lam_off * corr
            g = g.astype(bf16)
            gt[c, pl.ds(pl.multiple_of(base, 32), 32), :] = g
            prod = g.astype(f32) * corr
            lacc[...] += jnp.sum(ls_.reshape(4, 8, W), axis=0)
            csum = csum + jnp.sum(prod.reshape(4, 8, W), axis=0)
            racc[pl.ds(32 * h, 32), :] += total_of(
                [prod[:, t * 128:(t + 1) * 128] for t in range(W // 128)])
        for h in H:
            gather_early(gt.at[c], 512 * h + 128 * p1[h], p2[h], 32, nb2[h], "g2", c)
        pay[pl.ds(2 + k, 1), pl.ds(col(c), W)] = jnp.sum(csum, axis=0, keepdims=True)

    def f2(c):
        await_bytes(gt.at[c, pl.ds(0, 128)], ("g2", c, 0))
        for h in H:
            gather_late(gt.at[c], 512 * h + 128 * p1[h], p2[h], 32, nb2[h], "g2", c)

    def g1(c):
        await_bytes(gt.at[c, pl.ds(0, 64)], ("g2", c, 1))
        for h in H:
            gather_early(gt.at[c], 512 * h, p1[h], 128, nb1[h], "g1", c)

    def f1(c):
        await_bytes(gt.at[c, pl.ds(0, 512)], ("g1", c, 0))
        for h in H:
            gather_late(gt.at[c], 512 * h, p1[h], 128, nb1[h], "g1", c)

    started = []

    def bk(c):
        await_bytes(gt.at[c, pl.ds(0, 256)], ("g1", c, 1))
        k = blk(c)
        cs = pl.ds(col(c), W)
        j_ = c % CPK
        first = not started
        started.append(c)

        if k == 2:
            await_bytes(pbl.at[2, :, cs], ("p", 2, j_))
        v = jnp.dot(na[...], gt[c], preferred_element_type=f32)
        if k == 0:
            acc_b[:, cs] = v
        else:
            if k == 2:
                v = v + pbl[2, :, cs].astype(f32)
            pbs[k - 1, :, cs] = v.astype(bf16)
            send(pbs.at[k - 1, :, cs], pbl.at[k - 1, :, cs], ("p", k - 1, j_),
                 fdev[2] if k == 2 else fdev[1])
        u = lax.dot_general(bn[k, :, cs], gt[c], (((1,), (1,)), ((), ())),
                            preferred_element_type=f32)
        if first:
            acc_a[...] = u
        else:
            acc_a[...] += u

    def lo_send(base, me, to, value):
        lo[base + me] = value
        for q in to:
            send(lo.at[base + me], lo.at[base + me], ("l", base // 4), q)

    def lo_wait(base):
        await_bytes(lo.at[pl.ds(base, 3)], ("l", base // 4))
        return total_of([lo[base + q] for q in range(4)])

    def e0():
        pay[0:1, 0:W] = jnp.sum(lacc[...], axis=0, keepdims=True)
        rs = jnp.sum(racc[...], axis=1, keepdims=True)
        lanes = lax.broadcasted_iota(jnp.int32, (32, FB), 1)
        rows = lax.broadcasted_iota(jnp.int32, (32, FB), 0)
        spa = jnp.zeros((1, FB), f32)
        for h in H:
            here = lanes == base2(h) + rows
            spa = spa + jnp.sum(jnp.where(here, rs[32 * h:32 * h + 32], 0.0), axis=0, keepdims=True)
        pay[1:2, :] = spa
        lo_send(0, x, xto, pay[...])

    def e1():
        lo_send(4, y, yto, lo_wait(0))

    def e2():
        lo_send(8, fi, [fdev[1], fdev[2], fdev[3]], lo_wait(4))

    def e3():
        t = lo_wait(8)
        loss_ref[...] = jnp.full((8, 128), jnp.sum(t[0:1]), f32)

    def end():
        mine = [lo[8 + fidx[k]] for k in range(4)]
        m_a = mine[0][1:2]
        m_b = total_of([mine[k][2 + k:3 + k] for k in range(4)])
        v = unfold(vec[0])
        inv_a, inv_b = v[2:3], v[3:4]
        c_a = acc_a[ROWS:ROWS + 1, :] + acc_a[ROWS + 1:ROWS + 2, :]

        def finish_a(i, _):
            s = pl.ds(pl.multiple_of(i * 32, 32), 32)
            ga_ref[s, :] = inv_a * (acc_a[s, :] - c_a - na[s, :].astype(f32) * m_a)
            return 0

        lax.fori_loop(0, ROWS // 32, finish_a, 0)
        for j in range(CPK):
            cs = pl.ds(j * W, W)
            await_bytes(pbl.at[0, :, cs], ("p", 0, j))
            await_bytes(pbl.at[1, :, cs], ("p", 1, j))

        def back_b(s):
            return acc_b[s, :] + pbl[0, s, :].astype(f32) + pbl[1, s, :].astype(f32)

        c_b = back_b(pl.ds(ROWS, 16))
        c_b = c_b[0:1] + c_b[1:2]

        def finish_b(i, _):
            s = pl.ds(pl.multiple_of(i * 32, 32), 32)
            gb_ref[s, :] = inv_b * (back_b(s) - c_b - bn[0, s, :].astype(f32) * m_b)
            return 0

        lax.fori_loop(0, ROWS // 32, finish_b, 0)

    order = [
        (raw0,), (dot, 0), (s0,), (dot, 1), (dot, 2), (raw1,), (la, 0), (s1,), (la, 2), (la, 1),
        (dot, 3), (fa, 2), (fa, 0), (fa, 1), (s2,), (la, 3), (lb, 2), (lb, 0), (lb, 1), (fa, 3), (fr,),
        (dot, 4), (fb, 0), (lb, 3), (fb, 2), (la, 4), (dot, 6), (s3,), (fb, 3), (fa, 4), (la, 6),
        (dot, 5), (nm, 0), (fb, 1), (nm, 1), (lb, 4), (fa, 6), (dot, 7), (lb, 6), (fb, 4), (d0,),
        (la, 5), (nm, 3), (la, 7), (ti, 2), (fb, 6), (nm, 2), (ti, 4), (fa, 5), (ti, 0), (d1,),
        (fa, 7), (ti, 6), (f2, 4), (lb, 5), (f2, 2), (ti, 3), (lb, 7), (d2,), (f2, 6), (g1, 4),
        (fb, 5), (g1, 6), (fb, 7), (d3,), (ti, 1), (ti, 5), (ti, 7), (f1, 6), (f2, 0), (f2, 1), (d4,),
        (f2, 7), (f2, 5), (f2, 3), (f1, 4), (bk, 6), (g1, 7), (e0,), (g1, 5), (bk, 4), (f1, 7), (e1,),
        (g1, 3), (f1, 5), (g1, 2), (bk, 7), (e2,), (g1, 1), (f1, 3), (g1, 0), (bk, 5), (f1, 2),
        (f1, 1), (bk, 3), (f1, 0), (e3,), (bk, 2), (bk, 1), (bk, 0), (end,),
    ]
    for step, *args in order:
        step(*args)

    for region, name in (
        (mg.at[pl.ds(0, 48 + 192 + 256)], "m"), (mb.at[pl.ds(1, 3)], "n"),
        (db.at[pl.ds(1, 3), pl.ds(0, 32)], "w"), (ex2.at[pl.ds(0, 7)], "d"),
        (ld1, "r1"), (ld2, "r2"), (zbuf, "z"), (gt.at[:, pl.ds(0, 192)], "g2"),
        (gt.at[:, pl.ds(0, 768)], "g1"), (braw, "b"), (vec.at[pl.ds(1, 3)], "v"),
        (sbv.at[pl.ds(1, 3)], "f"), (pbl, "p"), (ex.at[pl.ds(0, 7)], "e"),
        (lo.at[pl.ds(0, 9)], "l"),
    ):
        await_sent(region, name)


def shards(view_a, view_b):
    vm = pl.BlockSpec(memory_space=pltpu.VMEM)
    dma = pltpu.SemaphoreType.DMA
    scratch = [
        pltpu.VMEM((RX, FB), bf16),
        pltpu.VMEM((FB, ROWS), bf16),
        pltpu.VMEM((4, RX, FB), bf16),
        pltpu.VMEM((3, ROWS, FB), bf16),
        pltpu.VMEM((NCH, FB, W), bf16),
        pltpu.VMEM((NCH, 12, 64, W), bf16),
        pltpu.VMEM((NCH, 2, 128, W), bf16),
        pltpu.VMEM((NCH, 12, 16, W), bf16),
        pltpu.VMEM((NCH, 64, W), bf16),
        pltpu.VMEM((NCH, 64, W), bf16),
        pltpu.VMEM((NCH, FB, W), bf16),
        pltpu.VMEM((3, RX, FB), bf16),
        pltpu.VMEM((3, RX, FB), bf16),
        pltpu.VMEM((RX, FB), f32),
        pltpu.VMEM((RX, FB), f32),
        pltpu.VMEM((10, 8, FB // 2), f32),
        pltpu.VMEM((10, 8, FB // 4), f32),
        pltpu.VMEM((32 * 16, 128), f32),
        pltpu.VMEM((4, 8, FB // 8), f32),
        pltpu.VMEM((4, 8, FB), f32),
        pltpu.VMEM((12, 8, FB), f32),
        pltpu.VMEM((8, FB), f32),
        pltpu.VMEM((4, 8, FB // 2), f32),
        pltpu.VMEM((4, 128, FB), bf16),
        pltpu.VMEM((FB, 128), f32),
        pltpu.VMEM((8, FB), f32),
        pltpu.VMEM((4, 8, FB // 4), f32),
        pltpu.VMEM((8, W), f32),
        pltpu.VMEM((64, 128), f32),
        dma((15,)),
        dma((NCH, 2)), dma((NCH, 2)), dma((NCH,)), dma((NCH, 2)), dma((NCH, 2)),
        dma((4,)), dma((3,)), dma((3,)), dma((1,)), dma((3, CPK)), dma((3,)), dma((3,)), dma((3,)),
        dma((3,)), dma((3,)),
    ]
    ga, gb, loss = pl.pallas_call(
        kernel,
        out_shape=(
            jax.ShapeDtypeStruct((ROWS, FB), f32),
            jax.ShapeDtypeStruct((ROWS, FB), f32),
            jax.ShapeDtypeStruct((8, 128), f32),
        ),
        in_specs=[vm, vm],
        out_specs=(vm, vm, vm),
        scratch_shapes=scratch,
        compiler_params=pltpu.CompilerParams(
            collective_id=0, has_side_effects=True, vmem_limit_bytes=60 * 2**20),
        name="barlow",
    )(view_a, view_b)
    return ga, gb, loss[0, 0]


def solution(mesh):
    return jax.shard_map(
        shards,
        mesh=mesh,
        in_specs=(P("batch", "feat"), P("batch", "feat")),
        out_specs=(P("batch", "feat"), P("batch", "feat"), P()),
        check_vma=False,
    )
```

```python
import jax
import jax.numpy as jnp
from jax import lax
from jax.experimental import pallas as pl
from jax.experimental.pallas import tpu as pltpu
from jax.sharding import PartitionSpec as P

lam_off = 0.0051
eps_norm = 1e-05
f32 = jnp.float32
bf16 = jnp.bfloat16
MESH = pl.DeviceIdType.MESH

ROWS = 512
RX = ROWS + 16
FB = 1024
CPK = 2
W = FB // CPK
NCH = 4 * CPK
TOTAL = 16384


def column_sum(fn, rows, step=32):
    def body(i, acc):
        v = fn(pl.ds(pl.multiple_of(i * step, step), step))
        return acc + jnp.sum(v.reshape(step // 8, 8, v.shape[-1]), axis=0)

    acc = lax.fori_loop(0, rows // step, body, jnp.zeros((8, FB), f32))
    return jnp.sum(acc, axis=0, keepdims=True)


def fold(v):
    w = v.shape[0] * FB // 8
    return jnp.concatenate([v[:, p * w:(p + 1) * w] for p in range(FB // w)], axis=0)


def unfold(v):
    r = v.shape[1] * 8 // FB
    return jnp.concatenate([v[p * r:(p + 1) * r] for p in range(8 // r)], axis=1)


def total_of(vs):
    t = vs[0]
    for v in vs[1:]:
        t = t + v
    return t


def kernel(
    a_ref, b_ref, ga_ref, gb_ref, loss_ref,
    na, nat, bn, braw, sb, ld1, sb2, ld2, ub, zbuf, gt, pbs, pbl, acc_a, acc_b,
    ex, ex2, mg, mb, mrow, lo, pay, vec, db, dat, dg, sbv, lacc, racc,
    ss, r1s, r2s, zs, g2s, g1s, bs, vs_, ws, fs, ps, es, e2s, ms, mbs, ls,
):
    bi = lax.axis_index("batch")
    fi = lax.axis_index("feat")
    y, zh, x = bi // 8, (bi // 4) % 2, bi % 4
    zl, core = fi // 2, fi % 2

    def dev(y_, zh_, x_, zl_, c_):
        return (((y_ + 4) % 4) * 8 + zh_ * 4 + ((x_ + 4) % 4), zl_ * 2 + c_)

    xdev = {d: dev(y, zh, x + d, zl, core) for d in (1, 2, 3)}
    ydev = {d: dev(y + d, zh, x, zl, core) for d in (1, 2, 3)}
    zhdev = dev(y, 1 - zh, x, zl, core)
    fdev = {1: dev(y, zh, x, zl, 1 - core), 2: dev(y, zh, x, 1 - zl, core),
            3: dev(y, zh, x, 1 - zl, 1 - core)}
    fidx = {0: fi, 1: zl * 2 + 1 - core, 2: (1 - zl) * 2 + core, 3: (1 - zl) * 2 + 1 - core}

    bar = pltpu.get_barrier_semaphore()
    partners = list(xdev.values()) + list(ydev.values()) + [zhdev] + list(fdev.values())
    for q in partners:
        pl.semaphore_signal(bar, inc=1, device_id=q, device_id_type=MESH)

    recv = {"r1": r1s, "r2": r2s, "z": zs, "g2": g2s, "g1": g1s, "b": bs, "v": vs_, "w": ws,
            "f": fs, "p": ps, "e": es, "d": e2s, "m": ms, "n": mbs, "l": ls}
    sent = {name: ss.at[i] for i, name in enumerate(recv)}

    def send(src, dst, key, to):
        cp = pltpu.make_async_remote_copy(
            src_ref=src, dst_ref=dst, send_sem=sent[key[0]], recv_sem=recv[key[0]].at[key[1:]],
            device_id=to, device_id_type=MESH)
        cp.start()

    def await_bytes(region, key):
        pltpu.make_async_remote_copy(
            src_ref=region, dst_ref=region, send_sem=sent[key[0]], recv_sem=recv[key[0]].at[key[1:]],
            device_id=zhdev, device_id_type=MESH).wait_recv()

    def await_sent(region, name):
        pltpu.make_async_remote_copy(
            src_ref=region, dst_ref=region, send_sem=sent[name], recv_sem=sent[name],
            device_id=zhdev, device_id_type=MESH).wait_send()

    def multiply(c, src):
        k = c // CPK
        o = c % CPK * W
        centered = (src[:, o:o + W].astype(f32) - mrow[k, 0:1, o:o + W]).astype(bf16)
        sb[c] = jnp.dot(nat[...], centered, preferred_element_type=f32).astype(bf16)

    mean_a = column_sum(lambda s: a_ref[s].astype(f32), ROWS) * (1.0 / ROWS)
    mean_b = column_sum(lambda s: b_ref[s].astype(f32), ROWS) * (1.0 / ROWS)

    mrow[0] = jnp.broadcast_to(mean_b, (8, FB))
    mb[0] = fold(mean_b)
    for i in range(4):
        s = slice(i * 256, (i + 1) * 256)
        nat[s, :] = (a_ref[:, s].astype(f32) - mean_a[:, s]).astype(bf16).T
    multiply(0, b_ref)

    def local_sums(i, acc):
        s = pl.ds(pl.multiple_of(i * 32, 32), 32)
        u = a_ref[s].astype(f32) - mean_a
        v = b_ref[s].astype(f32) - mean_b
        return tuple(t + jnp.sum(p.reshape(4, 8, FB), axis=0)
                     for t, p in zip(acc, (u * u, v * v, u * v)))

    z8 = jnp.zeros((8, FB), f32)
    local = [jnp.sum(t, axis=0, keepdims=True)
             for t in lax.fori_loop(0, ROWS // 32, local_sums, (z8, z8, z8))]
    lacc[...] = jnp.zeros_like(lacc)
    racc[...] = jnp.zeros_like(racc)
    pay[...] = jnp.zeros_like(pay)
    pl.semaphore_wait(bar, len(partners))

    xto = [xdev[d] for d in (1, 2, 3)]
    yto = [ydev[d] for d in (1, 2, 3)]
    axes = {"x": (0, 4, x, xto), "y": (4, 4, y, yto), "z": (8, 2, zh, [zhdev])}

    def ex_send(buf, name, axis, value):
        base, n, me, to = axes[axis]
        buf[base + me] = value
        for q in to:
            send(buf.at[base + me], buf.at[base + me], (name, base // 4), q)

    def ex_wait(buf, name, axis):
        base, n, me, to = axes[axis]
        await_bytes(buf.at[pl.ds(base, n - 1)], (name, base // 4))
        return total_of([buf[base + q] for q in range(n)])

    half = ROWS // 2

    def raw0():
        for k in (1, 2, 3):
            send(mb.at[0], mb.at[k], ("n", k - 1), fdev[k])
        send(b_ref, braw.at[0], ("b", 0), fdev[1])
        send(b_ref.at[pl.ds(0, half)], braw.at[1, pl.ds(0, half)], ("b", 1), fdev[2])

    def raw1():
        send(b_ref.at[pl.ds(half, half)], braw.at[1, pl.ds(half, half)], ("b", 2), fdev[2])

    def fr():
        for i in (0, 1):
            s = pl.ds(i * half, half)
            await_bytes(braw.at[1, s], ("b", 1 + i))
            send(braw.at[1, s], braw.at[2, s], ("b", 3), fdev[1])

    def group(n):
        return {1: (zh * 4 + y) * 4 + x, 4: (zh * 4 + y) * 4, 16: zh * 16}[n]

    def mg_send(n, axis):
        r = pl.ds(pl.multiple_of(group(n) * 16, 16), n * 16)
        for q in axes[axis][3]:
            send(mg.at[r], mg.at[r], ("m", axes[axis][0] // 4), q)

    def s0():
        mg[pl.ds(pl.multiple_of(group(1) * 16, 16), 16), :] = jnp.concatenate(
            [m[:, p * 128:(p + 1) * 128] for p in range(8) for m in (mean_a, mean_b)], axis=0)
        mg_send(1, "x")
        ex_send(ex, "e", "x", fold(jnp.concatenate(
            local + [jnp.zeros((1, FB), f32)], axis=0)))

    def s1():
        await_bytes(mg.at[pl.ds(0, 48)], ("m", 0))
        mg_send(4, "y")
        ex_send(ex, "e", "y", ex_wait(ex, "e", "x"))

    def s2():
        await_bytes(mg.at[pl.ds(0, 192)], ("m", 1))
        mg_send(16, "z")
        ex_send(ex, "e", "z", ex_wait(ex, "e", "y"))

    def s3():
        await_bytes(mg.at[pl.ds(0, 256)], ("m", 2))
        t = unfold(ex_wait(ex, "e", "z"))
        db[:, 32:128, :] = jnp.zeros((4, 96, FB), bf16)
        stat = []
        for p in range(8):
            s = slice(p * 128, (p + 1) * 128)
            da = mg[pl.ds(2 * p, 32, stride=16), :]
            dbb = mg[pl.ds(2 * p + 1, 32, stride=16), :]
            mu_a = jnp.sum(da, axis=0, keepdims=True) * (1.0 / 32)
            mu_b = jnp.sum(dbb, axis=0, keepdims=True) * (1.0 / 32)
            da = da - mu_a
            dbb = dbb - mu_b
            sq = [jnp.sum(u * v, axis=0, keepdims=True) * float(ROWS) + t[i:i + 1, s]
                  for i, (u, v) in enumerate(((da, da), (dbb, dbb), (da, dbb)))]
            inv_a = 1.0 / jnp.sqrt(sq[0] * (1.0 / TOTAL) + eps_norm)
            inv_b = 1.0 / jnp.sqrt(sq[1] * (1.0 / TOTAL) + eps_norm)
            stat.append(jnp.concatenate([mu_a, mu_b, inv_a, inv_b], axis=0))
            dg[:, s] = jnp.broadcast_to(sq[2] * (1.0 / TOTAL) * inv_a * inv_b, (8, 128))
            db[0, 0:32, s] = dbb.astype(bf16)
            dat[s, :] = jnp.concatenate([da, inv_a, jnp.zeros((95, 128), f32)], axis=0).T
        vec[0] = fold(jnp.concatenate(stat, axis=1))
        for k in (1, 2, 3):
            send(vec.at[0], vec.at[k], ("v", k - 1), fdev[k])
            send(db.at[0, pl.ds(0, 32)], db.at[k, pl.ds(0, 32)], ("w", k - 1), fdev[k])

    def normalise(src, dst, mean, iv):
        def body(i, _):
            s = pl.ds(pl.multiple_of(i * 64, 64), 64)
            dst[s, :] = ((src[s, :].astype(f32) - mean) * iv).astype(bf16)
            return 0
        lax.fori_loop(0, ROWS // 64, body, 0)

    def nm(k):
        if k > 0:
            await_bytes(vec.at[k], ("v", k - 1))
            await_bytes(db.at[k, pl.ds(0, 32)], ("w", k - 1))
        v = unfold(vec[k])
        normalise(braw.at[k - 1] if k else b_ref, bn.at[k], v[1:2], v[3:4])
        if k == 0:
            normalise(a_ref, na, v[0:1], v[2:3])

    def d0():
        s1_ = column_sum(lambda s: na[s].astype(f32), ROWS)
        s2_ = column_sum(lambda s: bn[0, s].astype(f32), ROWS)
        ex_send(ex2, "d", "x", fold(jnp.concatenate([s1_, s2_], axis=0)))

    def d1():
        ex_send(ex2, "d", "y", ex_wait(ex2, "d", "x"))

    def d2():
        ex_send(ex2, "d", "z", ex_wait(ex2, "d", "y"))

    def d3():
        sbv[0] = ex_wait(ex2, "d", "z") * (1.0 / TOTAL)
        for k in (1, 2, 3):
            send(sbv.at[0], sbv.at[k], ("f", 0), fdev[k])

    def d4():
        await_bytes(sbv.at[pl.ds(1, 3)], ("f", 0))
        rows = lax.broadcasted_iota(jnp.int32, (16, FB), 0)

        def two_terms(v):
            hi = v.astype(bf16).astype(f32)
            return jnp.where(rows == 0, hi, jnp.where(rows == 1, v - hi, 0.0)).astype(bf16)

        na[pl.ds(ROWS, 16), :] = two_terms(unfold(sbv[0])[0:1])
        for k in range(4):
            bn[k, pl.ds(ROWS, 16), :] = two_terms(unfold(sbv[k])[1:2])

    p1 = (x, y)
    p2 = (y, x)
    nb1 = ((xdev[1], xdev[3]), (ydev[1], ydev[3]))
    nb2 = (nb1[1], nb1[0])

    def at(q, d):
        return (q + d) % 4

    def piece(base, q, size, lo_, n):
        return pl.ds(pl.multiple_of(base + q * size + lo_, 16), n)

    def ring_early(buf, land, base, q, size, nb, name, c, first):
        hf = size // 2
        right, left = nb
        if first:
            send(buf.at[piece(base, at(q, 2), size, 0, hf)], land(0), (name, c, 0), right)
            send(buf.at[piece(base, at(q, 2), size, hf, hf)], land(1), (name, c, 0), left)
        else:
            send(buf.at[piece(base, at(q, 1), size, hf, hf)], land(2), (name, c, 1), right)
            send(buf.at[piece(base, at(q, 3), size, 0, hf)], land(3), (name, c, 1), left)

    def ring_late(buf, land, base, q, size, nb, name, c):
        hf = size // 2
        for m, p in ((0, piece(base, at(q, 1), size, 0, hf)),
                     (1, piece(base, at(q, 3), size, hf, hf))):
            buf[p, :] = (buf[p, :].astype(f32) + land(m)[...].astype(f32)).astype(bf16)
            send(buf.at[p], land(4 + m), (name, c, 1), nb[m])

    def ring_fin(buf, land, base, q, size, out, obase):
        hf = size // 2
        for lo_, u, v in ((0, 3, 4), (hf, 2, 5)):
            out[pl.ds(obase + lo_, hf), :] = (
                buf[piece(base, q, size, lo_, hf), :].astype(f32)
                + land(u)[...].astype(f32) + land(v)[...].astype(f32)).astype(bf16)

    def gather_early(buf, base, q, size, nb, name, c):
        own = buf.at[piece(base, q, size, 0, size)]
        for to in nb:
            send(own, own, (name, c, 0), to)

    def gather_late(buf, base, q, size, nb, name, c):
        hf = size // 2
        ha = buf.at[piece(base, at(q, 3), size, 0, hf)]
        hb = buf.at[piece(base, at(q, 1), size, hf, hf)]
        send(ha, ha, (name, c, 1), nb[0])
        send(hb, hb, (name, c, 1), nb[1])

    H = (0, 1)

    def blk(c):
        return c // CPK

    def col(c):
        return (c % CPK) * W

    def land1(c, h):
        return lambda m: ld1.at[c, (m * 2 + h)]

    def land2(c, h):
        return lambda m: ld2.at[c, (m * 2 + h)]

    def dot(c):
        k = blk(c)
        src = b_ref if k == 0 else braw.at[k - 1]
        if c % CPK == 0 and k > 0:
            if k == 1:
                await_bytes(braw.at[0], ("b", 0))
            if k == 3:
                await_bytes(braw.at[2], ("b", 3))
            await_bytes(mb.at[k], ("n", k - 1))
            mrow[k] = jnp.broadcast_to(unfold(mb[k]), (8, FB))
        if c > 0:
            multiply(c, src)
        for first in (True, False):
            for h in H:
                ring_early(sb.at[c], land1(c, h), 512 * h, p1[h], 128, nb1[h], "r1", c, first)

    def la(c):
        await_bytes(ld1.at[c, pl.ds(0, 4)], ("r1", c, 0))
        for h in H:
            ring_late(sb.at[c], land1(c, h), 512 * h, p1[h], 128, nb1[h], "r1", c)

    def fa(c):
        await_bytes(ld1.at[c, pl.ds(4, 8)], ("r1", c, 1))
        for h in H:
            ring_fin(sb.at[c], land1(c, h), 512 * h, p1[h], 128, sb2.at[c, h], 0)
        for first in (True, False):
            for h in H:
                ring_early(sb2.at[c, h], land2(c, h), 0, p2[h], 32, nb2[h], "r2", c, first)

    def lb(c):
        await_bytes(ld2.at[c, pl.ds(0, 4)], ("r2", c, 0))
        for h in H:
            ring_late(sb2.at[c, h], land2(c, h), 0, p2[h], 32, nb2[h], "r2", c)

    def fb(c):
        await_bytes(ld2.at[c, pl.ds(4, 8)], ("r2", c, 1))
        for h in H:
            ring_fin(sb2.at[c, h], land2(c, h), 0, p2[h], 32, ub.at[c], 32 * h)
        send(ub.at[c], zbuf.at[c], ("z", c), zhdev)

    def base2(h):
        return 512 * h + 128 * p1[h] + 32 * p2[h]

    def ti(c):
        await_bytes(zbuf.at[c], ("z", c))
        k = blk(c)
        csum = jnp.zeros((8, W), f32)
        inv_b = unfold(vec[k])[3:4, col(c):col(c) + W]
        for h in H:
            base = base2(h)
            mine = dat[pl.ds(pl.multiple_of(base, 32), 32), :]
            corr = (ub[c, pl.ds(32 * h, 32), :].astype(f32)
                    + zbuf[c, pl.ds(32 * h, 32), :].astype(f32)
                    + float(ROWS) * jnp.dot(mine.astype(bf16), db[k, :, col(c):col(c) + W],
                                            preferred_element_type=f32))
            corr = corr * (mine[:, 32:33] * (1.0 / TOTAL)) * inv_b
            if k == 0:
                diag = jnp.broadcast_to(dg[0:1, col(c):col(c) + W], (32, W))
                rows = base + lax.broadcasted_iota(jnp.int32, (32, W), 0)
                cols = col(c) + lax.broadcasted_iota(jnp.int32, (32, W), 1)
                on = rows == cols
                gap = 1.0 - diag
                corr = jnp.where(on, diag, corr)
                ls_ = jnp.where(on, gap * gap, lam_off * corr * corr)
                g = jnp.where(on, -2.0 * gap, 2.0 * lam_off * corr)
            else:
                ls_ = lam_off * corr * corr
                g = 2.0 * lam_off * corr
            g = g.astype(bf16)
            gt[c, pl.ds(pl.multiple_of(base, 32), 32), :] = g
            prod = g.astype(f32) * corr
            lacc[...] += jnp.sum(ls_.reshape(4, 8, W), axis=0)
            csum = csum + jnp.sum(prod.reshape(4, 8, W), axis=0)
            racc[pl.ds(32 * h, 32), :] += total_of(
                [prod[:, t * 128:(t + 1) * 128] for t in range(W // 128)])
        for h in H:
            gather_early(gt.at[c], 512 * h + 128 * p1[h], p2[h], 32, nb2[h], "g2", c)
        pay[pl.ds(2 + k, 1), pl.ds(col(c), W)] = jnp.sum(csum, axis=0, keepdims=True)

    def f2(c):
        await_bytes(gt.at[c, pl.ds(0, 128)], ("g2", c, 0))
        for h in H:
            gather_late(gt.at[c], 512 * h + 128 * p1[h], p2[h], 32, nb2[h], "g2", c)

    def g1(c):
        await_bytes(gt.at[c, pl.ds(0, 64)], ("g2", c, 1))
        for h in H:
            gather_early(gt.at[c], 512 * h, p1[h], 128, nb1[h], "g1", c)

    def f1(c):
        await_bytes(gt.at[c, pl.ds(0, 512)], ("g1", c, 0))
        for h in H:
            gather_late(gt.at[c], 512 * h, p1[h], 128, nb1[h], "g1", c)

    started = []

    def bk(c):
        await_bytes(gt.at[c, pl.ds(0, 256)], ("g1", c, 1))
        k = blk(c)
        cs = pl.ds(col(c), W)
        j_ = c % CPK
        first = not started
        started.append(c)

        if k == 2:
            await_bytes(pbl.at[2, :, cs], ("p", 2, j_))
        v = jnp.dot(na[...], gt[c], preferred_element_type=f32)
        if k == 0:
            acc_b[:, cs] = v
        else:
            if k == 2:
                v = v + pbl[2, :, cs].astype(f32)
            pbs[k - 1, :, cs] = v.astype(bf16)
            send(pbs.at[k - 1, :, cs], pbl.at[k - 1, :, cs], ("p", k - 1, j_),
                 fdev[2] if k == 2 else fdev[1])
        u = lax.dot_general(bn[k, :, cs], gt[c], (((1,), (1,)), ((), ())),
                            preferred_element_type=f32)
        if first:
            acc_a[...] = u
        else:
            acc_a[...] += u

    def lo_send(base, me, to, value):
        lo[base + me] = value
        for q in to:
            send(lo.at[base + me], lo.at[base + me], ("l", base // 4), q)

    def lo_wait(base):
        await_bytes(lo.at[pl.ds(base, 3)], ("l", base // 4))
        return total_of([lo[base + q] for q in range(4)])

    def e0():
        pay[0:1, 0:W] = jnp.sum(lacc[...], axis=0, keepdims=True)
        rs = jnp.sum(racc[...], axis=1, keepdims=True)
        lanes = lax.broadcasted_iota(jnp.int32, (32, FB), 1)
        rows = lax.broadcasted_iota(jnp.int32, (32, FB), 0)
        spa = jnp.zeros((1, FB), f32)
        for h in H:
            here = lanes == base2(h) + rows
            spa = spa + jnp.sum(jnp.where(here, rs[32 * h:32 * h + 32], 0.0), axis=0, keepdims=True)
        pay[1:2, :] = spa
        lo_send(0, x, xto, pay[...])

    def e1():
        lo_send(4, y, yto, lo_wait(0))

    def e2():
        lo_send(8, fi, [fdev[1], fdev[2], fdev[3]], lo_wait(4))

    def e3():
        t = lo_wait(8)
        loss_ref[...] = jnp.full((8, 128), jnp.sum(t[0:1]), f32)

    def end():
        mine = [lo[8 + fidx[k]] for k in range(4)]
        m_a = mine[0][1:2]
        m_b = total_of([mine[k][2 + k:3 + k] for k in range(4)])
        v = unfold(vec[0])
        inv_a, inv_b = v[2:3], v[3:4]
        c_a = acc_a[ROWS:ROWS + 1, :] + acc_a[ROWS + 1:ROWS + 2, :]

        def finish_a(i, _):
            s = pl.ds(pl.multiple_of(i * 32, 32), 32)
            ga_ref[s, :] = (
                inv_a * (acc_a[s, :] - c_a - na[s, :].astype(f32) * m_a)).astype(bf16)
            return 0

        lax.fori_loop(0, ROWS // 32, finish_a, 0)
        for j in range(CPK):
            cs = pl.ds(j * W, W)
            await_bytes(pbl.at[0, :, cs], ("p", 0, j))
            await_bytes(pbl.at[1, :, cs], ("p", 1, j))

        def back_b(s):
            return acc_b[s, :] + pbl[0, s, :].astype(f32) + pbl[1, s, :].astype(f32)

        c_b = back_b(pl.ds(ROWS, 16))
        c_b = c_b[0:1] + c_b[1:2]

        def finish_b(i, _):
            s = pl.ds(pl.multiple_of(i * 32, 32), 32)
            gb_ref[s, :] = (
                inv_b * (back_b(s) - c_b - bn[0, s, :].astype(f32) * m_b)).astype(bf16)
            return 0

        lax.fori_loop(0, ROWS // 32, finish_b, 0)

    order = [
        (raw0,), (raw1,), (dot, 0), (s0,), (dot, 1), (la, 0), (dot, 2), (la, 1), (s1,), (dot, 3),
        (fa, 1), (la, 3), (s2,), (fa, 0), (la, 2), (fa, 3), (lb, 0), (lb, 1), (fa, 2), (lb, 3), (fr,),
        (dot, 4), (lb, 2), (fb, 1), (fb, 0), (fb, 3), (la, 4), (dot, 6), (s3,), (fa, 4), (la, 6),
        (dot, 7), (lb, 4), (fb, 2), (nm, 0), (fa, 6), (dot, 5), (nm, 1), (fb, 4), (lb, 6), (la, 7),
        (nm, 3), (d0,), (nm, 2), (la, 5), (ti, 2), (fb, 6), (ti, 4), (fa, 7), (ti, 3), (d1,), (fa, 5),
        (ti, 6), (f2, 4), (ti, 1), (lb, 7), (lb, 5), (f2, 2), (d2,), (f2, 6), (g1, 4), (fb, 7),
        (g1, 6), (fb, 5), (d3,), (ti, 0), (ti, 7), (d4,), (ti, 5), (f1, 6), (f2, 7), (f2, 1), (f1, 4),
        (f2, 0), (f2, 3), (f2, 5), (bk, 6), (g1, 7), (e0,), (g1, 5), (bk, 4), (f1, 7), (g1, 3), (e1,),
        (f1, 5), (bk, 7), (g1, 2), (f1, 3), (g1, 1), (g1, 0), (e2,), (bk, 5), (f1, 2), (bk, 3), (e3,),
        (f1, 1), (f1, 0), (bk, 2), (bk, 1), (bk, 0), (end,),
    ]
    for step, *args in order:
        step(*args)

    for region, name in (
        (mg.at[pl.ds(0, 48 + 192 + 256)], "m"), (mb.at[pl.ds(1, 3)], "n"),
        (db.at[pl.ds(1, 3), pl.ds(0, 32)], "w"), (ex2.at[pl.ds(0, 7)], "d"),
        (ld1, "r1"), (ld2, "r2"), (zbuf, "z"), (gt.at[:, pl.ds(0, 192)], "g2"),
        (gt.at[:, pl.ds(0, 768)], "g1"), (braw, "b"), (vec.at[pl.ds(1, 3)], "v"),
        (sbv.at[pl.ds(1, 3)], "f"), (pbl, "p"), (ex.at[pl.ds(0, 7)], "e"),
        (lo.at[pl.ds(0, 9)], "l"),
    ):
        await_sent(region, name)


def shards(view_a, view_b):
    vm = pl.BlockSpec(memory_space=pltpu.VMEM)
    dma = pltpu.SemaphoreType.DMA
    scratch = [
        pltpu.VMEM((RX, FB), bf16),
        pltpu.VMEM((FB, ROWS), bf16),
        pltpu.VMEM((4, RX, FB), bf16),
        pltpu.VMEM((3, ROWS, FB), bf16),
        pltpu.VMEM((NCH, FB, W), bf16),
        pltpu.VMEM((NCH, 12, 64, W), bf16),
        pltpu.VMEM((NCH, 2, 128, W), bf16),
        pltpu.VMEM((NCH, 12, 16, W), bf16),
        pltpu.VMEM((NCH, 64, W), bf16),
        pltpu.VMEM((NCH, 64, W), bf16),
        pltpu.VMEM((NCH, FB, W), bf16),
        pltpu.VMEM((3, RX, FB), bf16),
        pltpu.VMEM((3, RX, FB), bf16),
        pltpu.VMEM((RX, FB), f32),
        pltpu.VMEM((RX, FB), f32),
        pltpu.VMEM((10, 8, FB // 2), f32),
        pltpu.VMEM((10, 8, FB // 4), f32),
        pltpu.VMEM((32 * 16, 128), f32),
        pltpu.VMEM((4, 8, FB // 8), f32),
        pltpu.VMEM((4, 8, FB), f32),
        pltpu.VMEM((12, 8, FB), f32),
        pltpu.VMEM((8, FB), f32),
        pltpu.VMEM((4, 8, FB // 2), f32),
        pltpu.VMEM((4, 128, FB), bf16),
        pltpu.VMEM((FB, 128), f32),
        pltpu.VMEM((8, FB), f32),
        pltpu.VMEM((4, 8, FB // 4), f32),
        pltpu.VMEM((8, W), f32),
        pltpu.VMEM((64, 128), f32),
        dma((15,)),
        dma((NCH, 2)), dma((NCH, 2)), dma((NCH,)), dma((NCH, 2)), dma((NCH, 2)),
        dma((4,)), dma((3,)), dma((3,)), dma((1,)), dma((3, CPK)), dma((3,)), dma((3,)), dma((3,)),
        dma((3,)), dma((3,)),
    ]
    ga, gb, loss = pl.pallas_call(
        kernel,
        out_shape=(
            jax.ShapeDtypeStruct((ROWS, FB), bf16),
            jax.ShapeDtypeStruct((ROWS, FB), bf16),
            jax.ShapeDtypeStruct((8, 128), f32),
        ),
        in_specs=[vm, vm],
        out_specs=(vm, vm, vm),
        scratch_shapes=scratch,
        compiler_params=pltpu.CompilerParams(
            collective_id=0, has_side_effects=True, vmem_limit_bytes=60 * 2**20),
        name="barlow",
    )(view_a, view_b)
    return ga.astype(f32), gb.astype(f32), loss[0, 0]


def solution(mesh):
    return jax.shard_map(
        shards,
        mesh=mesh,
        in_specs=(P("batch", "feat"), P("batch", "feat")),
        out_specs=(P("batch", "feat"), P("batch", "feat"), P()),
        check_vma=False,
    )
```

```python
import jax
import jax.numpy as jnp
from jax import lax
from jax.experimental import pallas as pl
from jax.experimental.pallas import tpu as pltpu
from jax.sharding import PartitionSpec as P

lam_off = 0.0051
eps_norm = 1e-05
f32 = jnp.float32
bf16 = jnp.bfloat16
MESH = pl.DeviceIdType.MESH

ROWS = 512
RX = ROWS + 16
FB = 1024
CPK = 2
W = FB // CPK
NCH = 4 * CPK
TOTAL = 16384


def column_sum(fn, rows, step=32):
    def body(i, acc):
        v = fn(pl.ds(pl.multiple_of(i * step, step), step))
        return acc + jnp.sum(v.reshape(step // 8, 8, v.shape[-1]), axis=0)

    acc = lax.fori_loop(0, rows // step, body, jnp.zeros((8, FB), f32))
    return jnp.sum(acc, axis=0, keepdims=True)


def fold(v):
    w = v.shape[0] * FB // 8
    return jnp.concatenate([v[:, p * w:(p + 1) * w] for p in range(FB // w)], axis=0)


def unfold(v):
    r = v.shape[1] * 8 // FB
    return jnp.concatenate([v[p * r:(p + 1) * r] for p in range(8 // r)], axis=1)


def total_of(vs):
    t = vs[0]
    for v in vs[1:]:
        t = t + v
    return t


def kernel(
    a_ref, b_ref, ga_ref, gb_ref, loss_ref,
    na, nat, bn, braw, sb, ld1, sb2, ld2, ub, zbuf, gt, pbs, pbl, acc_a, acc_b,
    ex, ex2, mg, mb, mrow, lo, pay, vec, db, dat, dg, sbv, lacc, racc,
    ss, r1s, r2s, zs, g2s, g1s, bs, vs_, ws, fs, ps, es, e2s, ms, mbs, ls,
):
    bi = lax.axis_index("batch")
    fi = lax.axis_index("feat")
    y, zh, x = bi // 8, (bi // 4) % 2, bi % 4
    zl, core = fi // 2, fi % 2

    def dev(y_, zh_, x_, zl_, c_):
        return (((y_ + 4) % 4) * 8 + zh_ * 4 + ((x_ + 4) % 4), zl_ * 2 + c_)

    xdev = {d: dev(y, zh, x + d, zl, core) for d in (1, 2, 3)}
    ydev = {d: dev(y + d, zh, x, zl, core) for d in (1, 2, 3)}
    zhdev = dev(y, 1 - zh, x, zl, core)
    fdev = {1: dev(y, zh, x, zl, 1 - core), 2: dev(y, zh, x, 1 - zl, core),
            3: dev(y, zh, x, 1 - zl, 1 - core)}
    fidx = {0: fi, 1: zl * 2 + 1 - core, 2: (1 - zl) * 2 + core, 3: (1 - zl) * 2 + 1 - core}

    bar = pltpu.get_barrier_semaphore()
    partners = list(xdev.values()) + list(ydev.values()) + [zhdev] + list(fdev.values())
    for q in partners:
        pl.semaphore_signal(bar, inc=1, device_id=q, device_id_type=MESH)

    recv = {"r1": r1s, "r2": r2s, "z": zs, "g2": g2s, "g1": g1s, "b": bs, "v": vs_, "w": ws,
            "f": fs, "p": ps, "e": es, "d": e2s, "m": ms, "n": mbs, "l": ls}
    sent = {name: ss.at[i] for i, name in enumerate(recv)}

    def send(src, dst, key, to):
        cp = pltpu.make_async_remote_copy(
            src_ref=src, dst_ref=dst, send_sem=sent[key[0]], recv_sem=recv[key[0]].at[key[1:]],
            device_id=to, device_id_type=MESH)
        cp.start()

    def await_bytes(region, key):
        pltpu.make_async_remote_copy(
            src_ref=region, dst_ref=region, send_sem=sent[key[0]], recv_sem=recv[key[0]].at[key[1:]],
            device_id=zhdev, device_id_type=MESH).wait_recv()

    def await_sent(region, name):
        pltpu.make_async_remote_copy(
            src_ref=region, dst_ref=region, send_sem=sent[name], recv_sem=sent[name],
            device_id=zhdev, device_id_type=MESH).wait_send()

    def multiply(c, src):
        k = c // CPK
        o = c % CPK * W
        centered = (src[:, o:o + W].astype(f32) - mrow[k, 0:1, o:o + W]).astype(bf16)
        sb[c] = jnp.dot(nat[...], centered, preferred_element_type=f32).astype(bf16)

    mean_a = column_sum(lambda s: a_ref[s].astype(f32), ROWS) * (1.0 / ROWS)
    mean_b = column_sum(lambda s: b_ref[s].astype(f32), ROWS) * (1.0 / ROWS)

    mrow[0] = jnp.broadcast_to(mean_b, (8, FB))
    mb[0] = fold(mean_b)
    for i in range(4):
        s = slice(i * 256, (i + 1) * 256)
        nat[s, :] = (a_ref[:, s].astype(f32) - mean_a[:, s]).astype(bf16).T
    multiply(0, b_ref)

    def local_sums(i, acc):
        s = pl.ds(pl.multiple_of(i * 32, 32), 32)
        u = a_ref[s].astype(f32) - mean_a
        v = b_ref[s].astype(f32) - mean_b
        return tuple(t + jnp.sum(p.reshape(4, 8, FB), axis=0)
                     for t, p in zip(acc, (u * u, v * v, u * v)))

    z8 = jnp.zeros((8, FB), f32)
    local = [jnp.sum(t, axis=0, keepdims=True)
             for t in lax.fori_loop(0, ROWS // 32, local_sums, (z8, z8, z8))]
    lacc[...] = jnp.zeros_like(lacc)
    racc[...] = jnp.zeros_like(racc)
    pay[...] = jnp.zeros_like(pay)
    pl.semaphore_wait(bar, len(partners))

    xto = [xdev[d] for d in (1, 2, 3)]
    yto = [ydev[d] for d in (1, 2, 3)]
    axes = {"x": (0, 4, x, xto), "y": (4, 4, y, yto), "z": (8, 2, zh, [zhdev])}

    def ex_send(buf, name, axis, value):
        base, n, me, to = axes[axis]
        buf[base + me] = value
        for q in to:
            send(buf.at[base + me], buf.at[base + me], (name, base // 4), q)

    def ex_wait(buf, name, axis):
        base, n, me, to = axes[axis]
        await_bytes(buf.at[pl.ds(base, n - 1)], (name, base // 4))
        return total_of([buf[base + q] for q in range(n)])

    half = ROWS // 2

    def raw0():
        for k in (1, 2, 3):
            send(mb.at[0], mb.at[k], ("n", k - 1), fdev[k])
        send(b_ref, braw.at[0], ("b", 0), fdev[1])
        send(b_ref.at[pl.ds(0, half)], braw.at[1, pl.ds(0, half)], ("b", 1), fdev[2])

    def raw1():
        send(b_ref.at[pl.ds(half, half)], braw.at[1, pl.ds(half, half)], ("b", 2), fdev[2])

    def fr():
        for i in (0, 1):
            s = pl.ds(i * half, half)
            await_bytes(braw.at[1, s], ("b", 1 + i))
            send(braw.at[1, s], braw.at[2, s], ("b", 3), fdev[1])

    def group(n):
        return {1: (zh * 4 + y) * 4 + x, 4: (zh * 4 + y) * 4, 16: zh * 16}[n]

    def mg_send(n, axis):
        r = pl.ds(pl.multiple_of(group(n) * 16, 16), n * 16)
        for q in axes[axis][3]:
            send(mg.at[r], mg.at[r], ("m", axes[axis][0] // 4), q)

    def s0():
        mg[pl.ds(pl.multiple_of(group(1) * 16, 16), 16), :] = jnp.concatenate(
            [m[:, p * 128:(p + 1) * 128] for p in range(8) for m in (mean_a, mean_b)], axis=0)
        mg_send(1, "x")
        ex_send(ex, "e", "x", fold(jnp.concatenate(
            local + [jnp.zeros((1, FB), f32)], axis=0)))

    def s1():
        await_bytes(mg.at[pl.ds(0, 48)], ("m", 0))
        mg_send(4, "y")
        ex_send(ex, "e", "y", ex_wait(ex, "e", "x"))

    def s2():
        await_bytes(mg.at[pl.ds(0, 192)], ("m", 1))
        mg_send(16, "z")
        ex_send(ex, "e", "z", ex_wait(ex, "e", "y"))

    def s3():
        await_bytes(mg.at[pl.ds(0, 256)], ("m", 2))
        t = unfold(ex_wait(ex, "e", "z"))
        db[:, 32:128, :] = jnp.zeros((4, 96, FB), bf16)
        stat = []
        for p in range(8):
            s = slice(p * 128, (p + 1) * 128)
            da = mg[pl.ds(2 * p, 32, stride=16), :]
            dbb = mg[pl.ds(2 * p + 1, 32, stride=16), :]
            mu_a = jnp.sum(da, axis=0, keepdims=True) * (1.0 / 32)
            mu_b = jnp.sum(dbb, axis=0, keepdims=True) * (1.0 / 32)
            da = da - mu_a
            dbb = dbb - mu_b
            sq = [jnp.sum(u * v, axis=0, keepdims=True) * float(ROWS) + t[i:i + 1, s]
                  for i, (u, v) in enumerate(((da, da), (dbb, dbb), (da, dbb)))]
            inv_a = 1.0 / jnp.sqrt(sq[0] * (1.0 / TOTAL) + eps_norm)
            inv_b = 1.0 / jnp.sqrt(sq[1] * (1.0 / TOTAL) + eps_norm)
            stat.append(jnp.concatenate([mu_a, mu_b, inv_a, inv_b], axis=0))
            dg[:, s] = jnp.broadcast_to(sq[2] * (1.0 / TOTAL) * inv_a * inv_b, (8, 128))
            db[0, 0:32, s] = dbb.astype(bf16)
            dat[s, :] = jnp.concatenate([da, inv_a, jnp.zeros((95, 128), f32)], axis=0).T
        vec[0] = fold(jnp.concatenate(stat, axis=1))
        for k in (1, 2, 3):
            send(vec.at[0], vec.at[k], ("v", k - 1), fdev[k])
            send(db.at[0, pl.ds(0, 32)], db.at[k, pl.ds(0, 32)], ("w", k - 1), fdev[k])

    def normalise(src, dst, mean, iv):
        def body(i, _):
            s = pl.ds(pl.multiple_of(i * 64, 64), 64)
            dst[s, :] = ((src[s, :].astype(f32) - mean) * iv).astype(bf16)
            return 0
        lax.fori_loop(0, ROWS // 64, body, 0)

    def nm(k):
        if k > 0:
            await_bytes(vec.at[k], ("v", k - 1))
            await_bytes(db.at[k, pl.ds(0, 32)], ("w", k - 1))
        v = unfold(vec[k])
        normalise(braw.at[k - 1] if k else b_ref, bn.at[k], v[1:2], v[3:4])
        if k == 0:
            normalise(a_ref, na, v[0:1], v[2:3])

    def d0():
        s1_ = column_sum(lambda s: na[s].astype(f32), ROWS)
        s2_ = column_sum(lambda s: bn[0, s].astype(f32), ROWS)
        ex_send(ex2, "d", "x", fold(jnp.concatenate([s1_, s2_], axis=0)))

    def d1():
        ex_send(ex2, "d", "y", ex_wait(ex2, "d", "x"))

    def d2():
        ex_send(ex2, "d", "z", ex_wait(ex2, "d", "y"))

    def d3():
        sbv[0] = ex_wait(ex2, "d", "z") * (1.0 / TOTAL)
        for k in (1, 2, 3):
            send(sbv.at[0], sbv.at[k], ("f", 0), fdev[k])

    def d4():
        await_bytes(sbv.at[pl.ds(1, 3)], ("f", 0))
        rows = lax.broadcasted_iota(jnp.int32, (16, FB), 0)

        def two_terms(v):
            hi = v.astype(bf16).astype(f32)
            return jnp.where(rows == 0, hi, jnp.where(rows == 1, v - hi, 0.0)).astype(bf16)

        na[pl.ds(ROWS, 16), :] = two_terms(unfold(sbv[0])[0:1])
        for k in range(4):
            bn[k, pl.ds(ROWS, 16), :] = two_terms(unfold(sbv[k])[1:2])

    p1 = (x, y)
    p2 = (y, x)
    nb1 = ((xdev[1], xdev[3]), (ydev[1], ydev[3]))
    nb2 = (nb1[1], nb1[0])

    def at(q, d):
        return (q + d) % 4

    def piece(base, q, size, lo_, n):
        return pl.ds(pl.multiple_of(base + q * size + lo_, 16), n)

    def ring_early(buf, land, base, q, size, nb, name, c, first):
        hf = size // 2
        right, left = nb
        if first:
            send(buf.at[piece(base, at(q, 2), size, 0, hf)], land(0), (name, c, 0), right)
            send(buf.at[piece(base, at(q, 2), size, hf, hf)], land(1), (name, c, 0), left)
        else:
            send(buf.at[piece(base, at(q, 1), size, hf, hf)], land(2), (name, c, 1), right)
            send(buf.at[piece(base, at(q, 3), size, 0, hf)], land(3), (name, c, 1), left)

    def ring_late(buf, land, base, q, size, nb, name, c):
        hf = size // 2
        for m, p in ((0, piece(base, at(q, 1), size, 0, hf)),
                     (1, piece(base, at(q, 3), size, hf, hf))):
            buf[p, :] = (buf[p, :].astype(f32) + land(m)[...].astype(f32)).astype(bf16)
            send(buf.at[p], land(4 + m), (name, c, 1), nb[m])

    def ring_fin(buf, land, base, q, size, out, obase):
        hf = size // 2
        for lo_, u, v in ((0, 3, 4), (hf, 2, 5)):
            out[pl.ds(obase + lo_, hf), :] = (
                buf[piece(base, q, size, lo_, hf), :].astype(f32)
                + land(u)[...].astype(f32) + land(v)[...].astype(f32)).astype(bf16)

    def gather_early(buf, base, q, size, nb, name, c):
        own = buf.at[piece(base, q, size, 0, size)]
        for to in nb:
            send(own, own, (name, c, 0), to)

    def gather_late(buf, base, q, size, nb, name, c):
        hf = size // 2
        ha = buf.at[piece(base, at(q, 3), size, 0, hf)]
        hb = buf.at[piece(base, at(q, 1), size, hf, hf)]
        send(ha, ha, (name, c, 1), nb[0])
        send(hb, hb, (name, c, 1), nb[1])

    H = (0, 1)

    def blk(c):
        return c // CPK

    def col(c):
        return (c % CPK) * W

    def land1(c, h):
        return lambda m: ld1.at[c, (m * 2 + h)]

    def land2(c, h):
        return lambda m: ld2.at[c, (m * 2 + h)]

    def dot(c):
        k = blk(c)
        src = b_ref if k == 0 else braw.at[k - 1]
        if c % CPK == 0 and k > 0:
            if k == 1:
                await_bytes(braw.at[0], ("b", 0))
            if k == 3:
                await_bytes(braw.at[2], ("b", 3))
            await_bytes(mb.at[k], ("n", k - 1))
            mrow[k] = jnp.broadcast_to(unfold(mb[k]), (8, FB))
        if c > 0:
            multiply(c, src)
        for first in (True, False):
            for h in H:
                ring_early(sb.at[c], land1(c, h), 512 * h, p1[h], 128, nb1[h], "r1", c, first)

    def la(c):
        await_bytes(ld1.at[c, pl.ds(0, 4)], ("r1", c, 0))
        for h in H:
            ring_late(sb.at[c], land1(c, h), 512 * h, p1[h], 128, nb1[h], "r1", c)

    def fa(c):
        await_bytes(ld1.at[c, pl.ds(4, 8)], ("r1", c, 1))
        for h in H:
            ring_fin(sb.at[c], land1(c, h), 512 * h, p1[h], 128, sb2.at[c, h], 0)
        for first in (True, False):
            for h in H:
                ring_early(sb2.at[c, h], land2(c, h), 0, p2[h], 32, nb2[h], "r2", c, first)

    def lb(c):
        await_bytes(ld2.at[c, pl.ds(0, 4)], ("r2", c, 0))
        for h in H:
            ring_late(sb2.at[c, h], land2(c, h), 0, p2[h], 32, nb2[h], "r2", c)

    def fb(c):
        await_bytes(ld2.at[c, pl.ds(4, 8)], ("r2", c, 1))
        for h in H:
            ring_fin(sb2.at[c, h], land2(c, h), 0, p2[h], 32, ub.at[c], 32 * h)
        send(ub.at[c], zbuf.at[c], ("z", c), zhdev)

    def base2(h):
        return 512 * h + 128 * p1[h] + 32 * p2[h]

    def ti(c):
        await_bytes(zbuf.at[c], ("z", c))
        k = blk(c)
        csum = jnp.zeros((8, W), f32)
        inv_b = unfold(vec[k])[3:4, col(c):col(c) + W]
        for h in H:
            base = base2(h)
            mine = dat[pl.ds(pl.multiple_of(base, 32), 32), :]
            corr = (ub[c, pl.ds(32 * h, 32), :].astype(f32)
                    + zbuf[c, pl.ds(32 * h, 32), :].astype(f32)
                    + float(ROWS) * jnp.dot(mine.astype(bf16), db[k, :, col(c):col(c) + W],
                                            preferred_element_type=f32))
            corr = corr * (mine[:, 32:33] * (1.0 / TOTAL)) * inv_b
            if k == 0:
                diag = jnp.broadcast_to(dg[0:1, col(c):col(c) + W], (32, W))
                rows = base + lax.broadcasted_iota(jnp.int32, (32, W), 0)
                cols = col(c) + lax.broadcasted_iota(jnp.int32, (32, W), 1)
                on = rows == cols
                gap = 1.0 - diag
                corr = jnp.where(on, diag, corr)
                ls_ = jnp.where(on, gap * gap, lam_off * corr * corr)
                g = jnp.where(on, -2.0 * gap, 2.0 * lam_off * corr)
            else:
                ls_ = lam_off * corr * corr
                g = 2.0 * lam_off * corr
            g = g.astype(bf16)
            gt[c, pl.ds(pl.multiple_of(base, 32), 32), :] = g
            prod = g.astype(f32) * corr
            lacc[...] += jnp.sum(ls_.reshape(4, 8, W), axis=0)
            csum = csum + jnp.sum(prod.reshape(4, 8, W), axis=0)
            racc[pl.ds(32 * h, 32), :] += total_of(
                [prod[:, t * 128:(t + 1) * 128] for t in range(W // 128)])
        for h in H:
            gather_early(gt.at[c], 512 * h + 128 * p1[h], p2[h], 32, nb2[h], "g2", c)
        pay[pl.ds(2 + k, 1), pl.ds(col(c), W)] = jnp.sum(csum, axis=0, keepdims=True)

    def f2(c):
        await_bytes(gt.at[c, pl.ds(0, 128)], ("g2", c, 0))
        for h in H:
            gather_late(gt.at[c], 512 * h + 128 * p1[h], p2[h], 32, nb2[h], "g2", c)

    def g1(c):
        await_bytes(gt.at[c, pl.ds(0, 64)], ("g2", c, 1))
        for h in H:
            gather_early(gt.at[c], 512 * h, p1[h], 128, nb1[h], "g1", c)

    def f1(c):
        await_bytes(gt.at[c, pl.ds(0, 512)], ("g1", c, 0))
        for h in H:
            gather_late(gt.at[c], 512 * h, p1[h], 128, nb1[h], "g1", c)

    started = []

    def bk(c):
        await_bytes(gt.at[c, pl.ds(0, 256)], ("g1", c, 1))
        k = blk(c)
        cs = pl.ds(col(c), W)
        j_ = c % CPK
        first = not started
        started.append(c)

        if k == 2:
            await_bytes(pbl.at[2, :, cs], ("p", 2, j_))
        v = jnp.dot(na[...], gt[c], preferred_element_type=f32)
        if k == 0:
            acc_b[:, cs] = v
        else:
            if k == 2:
                v = v + pbl[2, :, cs].astype(f32)
            pbs[k - 1, :, cs] = v.astype(bf16)
            send(pbs.at[k - 1, :, cs], pbl.at[k - 1, :, cs], ("p", k - 1, j_),
                 fdev[2] if k == 2 else fdev[1])
        u = lax.dot_general(bn[k, :, cs], gt[c], (((1,), (1,)), ((), ())),
                            preferred_element_type=f32)
        if first:
            acc_a[...] = u
        else:
            acc_a[...] += u

    def lo_send(base, me, to, value):
        lo[base + me] = value
        for q in to:
            send(lo.at[base + me], lo.at[base + me], ("l", base // 4), q)

    def lo_wait(base):
        await_bytes(lo.at[pl.ds(base, 3)], ("l", base // 4))
        return total_of([lo[base + q] for q in range(4)])

    def e0():
        pay[0:1, 0:W] = jnp.sum(lacc[...], axis=0, keepdims=True)
        rs = jnp.sum(racc[...], axis=1, keepdims=True)
        lanes = lax.broadcasted_iota(jnp.int32, (32, FB), 1)
        rows = lax.broadcasted_iota(jnp.int32, (32, FB), 0)
        spa = jnp.zeros((1, FB), f32)
        for h in H:
            here = lanes == base2(h) + rows
            spa = spa + jnp.sum(jnp.where(here, rs[32 * h:32 * h + 32], 0.0), axis=0, keepdims=True)
        pay[1:2, :] = spa
        lo_send(0, x, xto, pay[...])

    def e1():
        lo_send(4, y, yto, lo_wait(0))

    def e2():
        lo_send(8, fi, [fdev[1], fdev[2], fdev[3]], lo_wait(4))

    def e3():
        t = lo_wait(8)
        loss_ref[...] = jnp.full((8, 128), jnp.sum(t[0:1]), f32)

    def end():
        mine = [lo[8 + fidx[k]] for k in range(4)]
        m_a = mine[0][1:2]
        m_b = total_of([mine[k][2 + k:3 + k] for k in range(4)])
        v = unfold(vec[0])
        inv_a, inv_b = v[2:3], v[3:4]
        c_a = acc_a[ROWS:ROWS + 1, :] + acc_a[ROWS + 1:ROWS + 2, :]

        def finish_a(i, _):
            s = pl.ds(pl.multiple_of(i * 32, 32), 32)
            ga_ref[s, :] = (
                inv_a * (acc_a[s, :] - c_a - na[s, :].astype(f32) * m_a)).astype(bf16)
            return 0

        lax.fori_loop(0, ROWS // 32, finish_a, 0)
        for j in range(CPK):
            cs = pl.ds(j * W, W)
            await_bytes(pbl.at[0, :, cs], ("p", 0, j))
            await_bytes(pbl.at[1, :, cs], ("p", 1, j))

        def back_b(s):
            return acc_b[s, :] + pbl[0, s, :].astype(f32) + pbl[1, s, :].astype(f32)

        c_b = back_b(pl.ds(ROWS, 16))
        c_b = c_b[0:1] + c_b[1:2]

        def finish_b(i, _):
            s = pl.ds(pl.multiple_of(i * 32, 32), 32)
            gb_ref[s, :] = (
                inv_b * (back_b(s) - c_b - bn[0, s, :].astype(f32) * m_b)).astype(bf16)
            return 0

        lax.fori_loop(0, ROWS // 32, finish_b, 0)

    order = [
        (raw0,), (raw1,), (dot, 0), (s0,), (dot, 1), (dot, 2), (la, 1), (s1,), (la, 2), (la, 0),
        (dot, 3), (fa, 2), (s2,), (fa, 0), (fa, 1), (la, 3), (lb, 2), (lb, 0), (lb, 1), (fr,),
        (dot, 4), (fb, 2), (fb, 1), (fa, 3), (fb, 0), (dot, 6), (la, 4), (s3,), (la, 6), (nm, 1),
        (dot, 7), (nm, 0), (nm, 2), (fa, 6), (fa, 4), (ti, 0), (lb, 3), (d0,), (lb, 6), (la, 7),
        (lb, 4), (dot, 5), (fb, 6), (f2, 0), (nm, 3), (fb, 4), (fa, 7), (la, 5), (ti, 6), (ti, 1),
        (lb, 7), (fb, 3), (ti, 4), (fa, 5), (f2, 6), (ti, 2), (d1,), (fb, 7), (f2, 4), (f2, 1),
        (lb, 5), (g1, 6), (g1, 4), (d2,), (fb, 5), (ti, 7), (f1, 6), (d3,), (f2, 2), (ti, 5), (f2, 7),
        (f1, 4), (ti, 3), (d4,), (bk, 6), (f2, 5), (g1, 7), (e0,), (f2, 3), (g1, 5), (bk, 4), (f1, 7),
        (g1, 3), (e1,), (f1, 5), (g1, 2), (bk, 7), (e2,), (g1, 1), (bk, 5), (f1, 3), (g1, 0), (f1, 2),
        (e3,), (bk, 3), (f1, 1), (f1, 0), (bk, 2), (bk, 1), (bk, 0), (end,),
    ]
    for step, *args in order:
        step(*args)

    for region, name in (
        (mg.at[pl.ds(0, 48 + 192 + 256)], "m"), (mb.at[pl.ds(1, 3)], "n"),
        (db.at[pl.ds(1, 3), pl.ds(0, 32)], "w"), (ex2.at[pl.ds(0, 7)], "d"),
        (ld1, "r1"), (ld2, "r2"), (zbuf, "z"), (gt.at[:, pl.ds(0, 192)], "g2"),
        (gt.at[:, pl.ds(0, 768)], "g1"), (braw, "b"), (vec.at[pl.ds(1, 3)], "v"),
        (sbv.at[pl.ds(1, 3)], "f"), (pbl, "p"), (ex.at[pl.ds(0, 7)], "e"),
        (lo.at[pl.ds(0, 9)], "l"),
    ):
        await_sent(region, name)


def widen(a_ref, b_ref, l_ref, ga_ref, gb_ref, loss_ref):
    ga_ref[...] = a_ref[...].astype(f32)
    gb_ref[...] = b_ref[...].astype(f32)
    loss_ref[...] = l_ref[0:1, 0:1]


def shards(view_a, view_b):
    vm = pl.BlockSpec(memory_space=pltpu.VMEM)
    dma = pltpu.SemaphoreType.DMA
    scratch = [
        pltpu.VMEM((RX, FB), bf16),
        pltpu.VMEM((FB, ROWS), bf16),
        pltpu.VMEM((4, RX, FB), bf16),
        pltpu.VMEM((3, ROWS, FB), bf16),
        pltpu.VMEM((NCH, FB, W), bf16),
        pltpu.VMEM((NCH, 12, 64, W), bf16),
        pltpu.VMEM((NCH, 2, 128, W), bf16),
        pltpu.VMEM((NCH, 12, 16, W), bf16),
        pltpu.VMEM((NCH, 64, W), bf16),
        pltpu.VMEM((NCH, 64, W), bf16),
        pltpu.VMEM((NCH, FB, W), bf16),
        pltpu.VMEM((3, RX, FB), bf16),
        pltpu.VMEM((3, RX, FB), bf16),
        pltpu.VMEM((RX, FB), f32),
        pltpu.VMEM((RX, FB), f32),
        pltpu.VMEM((10, 8, FB // 2), f32),
        pltpu.VMEM((10, 8, FB // 4), f32),
        pltpu.VMEM((32 * 16, 128), f32),
        pltpu.VMEM((4, 8, FB // 8), f32),
        pltpu.VMEM((4, 8, FB), f32),
        pltpu.VMEM((12, 8, FB), f32),
        pltpu.VMEM((8, FB), f32),
        pltpu.VMEM((4, 8, FB // 2), f32),
        pltpu.VMEM((4, 128, FB), bf16),
        pltpu.VMEM((FB, 128), f32),
        pltpu.VMEM((8, FB), f32),
        pltpu.VMEM((4, 8, FB // 4), f32),
        pltpu.VMEM((8, W), f32),
        pltpu.VMEM((64, 128), f32),
        dma((15,)),
        dma((NCH, 2)), dma((NCH, 2)), dma((NCH,)), dma((NCH, 2)), dma((NCH, 2)),
        dma((4,)), dma((3,)), dma((3,)), dma((1,)), dma((3, CPK)), dma((3,)), dma((3,)), dma((3,)),
        dma((3,)), dma((3,)),
    ]
    ga, gb, loss = pl.pallas_call(
        kernel,
        out_shape=(
            jax.ShapeDtypeStruct((ROWS, FB), bf16),
            jax.ShapeDtypeStruct((ROWS, FB), bf16),
            jax.ShapeDtypeStruct((8, 128), f32),
        ),
        in_specs=[vm, vm],
        out_specs=(vm, vm, vm),
        scratch_shapes=scratch,
        compiler_params=pltpu.CompilerParams(
            collective_id=0, has_side_effects=True, vmem_limit_bytes=60 * 2**20),
        name="barlow",
    )(view_a, view_b)
    n = 4
    block = pl.BlockSpec((ROWS // n, FB), lambda i: (i, 0))
    one = pl.BlockSpec((1, 1), lambda i: (0, 0))
    ga, gb, loss = pl.pallas_call(
        widen,
        grid=(n,),
        out_shape=(
            jax.ShapeDtypeStruct((ROWS, FB), f32),
            jax.ShapeDtypeStruct((ROWS, FB), f32),
            jax.ShapeDtypeStruct((1, 1), f32),
        ),
        in_specs=[block, block, pl.BlockSpec((8, 128), lambda i: (0, 0))],
        out_specs=(block, block, one),
        compiler_params=pltpu.CompilerParams(vmem_limit_bytes=60 * 2**20),
        name="widen",
    )(ga, gb, loss)
    return ga, gb, loss[0, 0]


def solution(mesh):
    return jax.shard_map(
        shards,
        mesh=mesh,
        in_specs=(P("batch", "feat"), P("batch", "feat")),
        out_specs=(P("batch", "feat"), P("batch", "feat"), P()),
        check_vma=False,
    )
```
